128 devices in a mesh: fsdp: 32 (over z, y_lo, x), tp: 4 (over y_hi, core).
Axes of the slice: x: 4, y: 4 (y_hi: 2, y_lo: 2; y = y_hi * 2 + y_lo), z: 4, core: 2. Of those that a mesh axis runs over, the one named last changes fastest.
Arguments:
- acts: bfloat16 [4096, 4096], P('fsdp', 'tp'), may hold values from -6 to 6
- gate_codes: int32 [14336, 4096], P('fsdp', 'tp'), may hold values from -8 to 7
- gate_scales: float32 [14336, 32], P('fsdp', 'tp'), may hold values from 0.0015 to 0.006
- up_codes: int32 [14336, 4096], P('fsdp', 'tp'), may hold values from -8 to 7
- up_scales: float32 [14336, 32], P('fsdp', 'tp'), may hold values from 0.0015 to 0.006
- down_codes: int32 [14336, 4096], P('fsdp', 'tp'), may hold values from -8 to 7
- down_scales: float32 [14336, 32], P('fsdp', 'tp'), may hold values from 0.0009 to 0.0036
- cotangent: bfloat16 [4096, 4096], P('fsdp', 'tp'), may hold values from -0.099609375 to 0.099609375
Outputs:
- output: bfloat16 [4096, 4096], P('fsdp', 'tp')
- grad_gate: float32 [14336, 4096], P('fsdp', 'tp')
- grad_up: float32 [14336, 4096], P('fsdp', 'tp')
- grad_down: float32 [14336, 4096], P('fsdp', 'tp')
The draws below stay inside these ranges and needn't reach their ends.
All inputs are finite; a program needn't handle non-finite values.
Results may differ from the reference program's by a relative error of at most 0.035.
Values may be sent and summed in bfloat16 or wider, within the bound.
A program may use at most 128 MiB of HBM per device.

```python
import math
import jax
import jax.numpy as jnp
from jax import lax

D = 4096
FF = 14336
GROUP = 128
TOKENS = 4096
DSLICE = 1024
FSLICE = 448
N_FSDP = 32
N_TP = 4


def touch_ends(result, own_key, least, high):
    place = [jax.random.randint(jax.random.fold_in(own_key, axis), (), 0, length) for axis, length in enumerate(result.shape)]
    main_axis = result.shape.index(max(result.shape))
    beside = place[:main_axis] + [(place[main_axis] + 1) % result.shape[main_axis]] + place[main_axis + 1:]
    return result.at[tuple(place)].set(least).at[tuple(beside)].set(high)


def steps_of(stream_key, shape, pieces, least, high):
    def one(position, parts):
        steps = jax.random.uniform(jax.random.fold_in(jax.random.fold_in(stream_key, 6), position), (parts,), jnp.float32, least / len(pieces), high / len(pieces))
        return jnp.repeat(jnp.exp(steps), shape[position] // parts).reshape((-1,) + (1,) * (len(shape) - position - 1))

    loudness = one(*pieces[0])
    for cut in pieces[1:]:
        loudness = loudness * one(*cut)
    return loudness


def centred(rng, shape, deviation, reach, shards=(), kind=jnp.bfloat16):
    level = steps_of(rng, shape, shards, -0.22, 0.18) if shards else 1.0
    drawn = jax.random.normal(rng, shape, jnp.float32) * deviation * level
    return jnp.minimum(jnp.maximum(drawn, -reach), reach).astype(kind)


def setup_inputs(seed: int = 0) -> dict:
    seeds = jax.random.split(jax.random.key(seed), 9)
    acts = centred(seeds[0], (TOKENS, D), 1.0, 6.0, ((0, 32), (1, 4)))
    gate_codes = touch_ends(jax.random.randint(seeds[1], (FF, D), -8, 8), jax.random.fold_in(seeds[1], 1), -8, 7).astype(jnp.int32)
    gate_scales = jnp.clip(jnp.exp(math.log(0.006) - 1.3862944 * jax.random.uniform(seeds[2], (FF, D // GROUP), jnp.float32) ** steps_of(seeds[2], (FF, D // GROUP), ((0, 32), (1, 4)), -0.2, 0.2)), 0.0015, 0.006)
    up_codes = touch_ends(jax.random.randint(seeds[3], (FF, D), -8, 8), jax.random.fold_in(seeds[3], 1), -8, 7).astype(jnp.int32)
    up_scales = jnp.clip(jnp.exp(math.log(0.006) - 1.3862944 * jax.random.uniform(seeds[4], (FF, D // GROUP), jnp.float32) ** steps_of(seeds[4], (FF, D // GROUP), ((0, 32), (1, 4)), -0.2, 0.2)), 0.0015, 0.006)
    down_codes = touch_ends(jax.random.randint(seeds[5], (FF, D), -8, 8), jax.random.fold_in(seeds[5], 1), -8, 7).astype(jnp.int32)
    down_scales = jnp.clip(jnp.exp(math.log(0.0036) - 1.3862944 * jax.random.uniform(seeds[6], (FF, D // GROUP), jnp.float32) ** steps_of(seeds[6], (FF, D // GROUP), ((0, 32), (1, 4)), -0.2, 0.2)), 0.0009, 0.0036)
    cotangent = centred(seeds[7], (TOKENS, D), 0.0156, 0.099609375, ((0, 32), (1, 4)))
    return dict(acts=acts, gate_codes=gate_codes, gate_scales=gate_scales, up_codes=up_codes, up_scales=up_scales, down_codes=down_codes, down_scales=down_scales, cotangent=cotangent)


def dequantize(code_values, scale_values):
    num_rows, num_cols = code_values.shape
    grouped = code_values.astype(jnp.float32).reshape(num_rows, num_cols // GROUP, GROUP) * scale_values[:, :, None]
    return grouped.reshape(num_rows, num_cols).astype(jnp.bfloat16)


def rounded(product):
    narrow = lax.optimization_barrier(product.astype(jnp.bfloat16))
    return narrow.astype(jnp.float32)


def contract_last(left_side, right_side):
    return lax.dot_general(left_side, right_side, (((1,), (1,)), ((), ())), preferred_element_type=jnp.float32)


def contract_first(left_side, right_side):
    return lax.dot_general(left_side, right_side, (((0,), (0,)), ((), ())), preferred_element_type=jnp.float32)


def silu_slope(values):
    logistic = jax.nn.sigmoid(values)
    return logistic * (1.0 + values * (1.0 - logistic))


def feature_blocks(left_side, weight):
    running = jnp.zeros((left_side.shape[0], weight.shape[0]), jnp.float32)
    for block_index in range(N_TP):
        first_col = block_index * DSLICE
        running = running + rounded(contract_last(left_side[:, first_col:first_col + DSLICE], weight[:, first_col:first_col + DSLICE]))
    return running


def hidden_blocks(hidden, w_down):
    hidden_split = hidden.reshape(TOKENS, N_FSDP, FSLICE).transpose(1, 0, 2)
    weight_split = w_down.reshape(N_FSDP, FSLICE, D)

    def accumulate(running, members):
        hidden_part, weight_part = members
        return running + rounded(jnp.dot(hidden_part, weight_part, preferred_element_type=jnp.float32)), None

    running, unused = lax.scan(accumulate, jnp.zeros((TOKENS, D), jnp.float32), (hidden_split, weight_split))
    return running


def reference(acts, gate_codes, gate_scales, up_codes, up_scales, down_codes, down_scales, cotangent):
    w_gate = dequantize(gate_codes, gate_scales)
    w_up = dequantize(up_codes, up_scales)
    w_down = dequantize(down_codes, down_scales)
    gate = feature_blocks(acts, w_gate)
    up = feature_blocks(acts, w_up)
    hidden = (jax.nn.silu(gate) * up).astype(jnp.bfloat16)
    output = hidden_blocks(hidden, w_down).astype(jnp.bfloat16)
    grad_hidden = feature_blocks(cotangent, w_down)
    grad_gate_act = (grad_hidden * up * silu_slope(gate)).astype(jnp.bfloat16)
    grad_up_act = (grad_hidden * jax.nn.silu(gate)).astype(jnp.bfloat16)
    grad_gate = contract_first(grad_gate_act, acts)
    grad_up = contract_first(grad_up_act, acts)
    grad_down = contract_first(hidden, cotangent)
    return output, grad_gate, grad_up, grad_down
```

```python
import functools

import jax
import jax.numpy as jnp
from jax import lax
from jax.experimental import pallas as pl
from jax.experimental.pallas import tpu as pltpu
from jax.sharding import PartitionSpec as P

MESH = pl.DeviceIdType.MESH
F32, BF16 = jnp.float32, jnp.bfloat16
GROUP = 128
HID = 448
HALF = 1024
WIDE = 2 * HALF
BLK = 64
CH = 256
DELTAS = (1, 3, 2)

ACTS, COT, WTS, TFGU, TFGH, RSB, RSA, RSY, OUTS, GRD, GRU, NSEM = 0, 14, 28, 31, 39, 47, 53, 56, 57, 58, 59, 60
SIB, YLO, AOWN, ALO, BH = 0, 1, 2, 5, 8


def nt(left, right):
    return lax.dot_general(left, right, (((1,), (1,)), ((), ())), preferred_element_type=F32)


def nn(left, right):
    return lax.dot_general(left, right, (((1,), (0,)), ((), ())), preferred_element_type=F32)


def kernel(acts, gc, gs, uc, us, dc, ds, cot, out, gg, gu, gd,
           A, C, W2, WD, TO, TR, O, RB, RA, RY, HT, DS, DR, ssem, rsem, lsem, credit):
    f, t = lax.axis_index("fsdp"), lax.axis_index("tp")
    x, ylo, z = f % 4, (f // 4) % 2, f // 8
    yhi, c = t // 2, t % 2
    a = x * (1 - c) + z * c
    b = z * (1 - c) + x * c

    def dev(x_, ylo_, z_, yhi_, c_):
        return (z_ * 8 + ylo_ * 4 + x_, yhi_ * 2 + c_)

    def apeer(d):
        return dev((x + d * (1 - c)) % 4, ylo, (z + d * c) % 4, yhi, c)

    def bpeer(d):
        return dev((x + d * c) % 4, ylo, (z + d * (1 - c)) % 4, yhi, c)

    sib = dev(x, ylo, z, yhi, 1 - c)
    lo = dev(x, 1 - ylo, z, yhi, c)
    hi = dev(x, ylo, z, 1 - yhi, c)

    def rc(src, dst, s, r, to):
        return pltpu.make_async_remote_copy(src_ref=src, dst_ref=dst, send_sem=ssem.at[s], recv_sem=rsem.at[r],
                                            device_id=to, device_id_type=MESH)

    def send(src, dst, s, r, to):
        rc(src, dst, s, r, to).start()

    def got(dst, r, to):
        rc(dst, dst, 0, r, to).wait_recv()

    def sent(src, s, to):
        rc(src, src, s, 0, to).wait_send()

    def blk(a_, ylo_):
        return pl.ds(pl.multiple_of(((b * 4 + a_) * 2 + ylo_) * BLK, BLK), BLK)

    def pair(a_):
        return pl.ds(pl.multiple_of((b * 4 + a_) * 2 * BLK, 2 * BLK), 2 * BLK)

    def chunk(b_, h):
        return b_ * 2 + h

    def rows(k):
        return pl.ds(pl.multiple_of(k * CH, CH), CH)

    def bd(j):
        return (b + 1 + 2 * j - 3 * (j // 2)) % 4

    mine = pl.ds(pl.multiple_of(c * BLK, BLK), BLK)
    theirs = pl.ds(pl.multiple_of((1 - c) * BLK, BLK), BLK)
    own = blk(a, ylo)
    other = blk(a, 1 - ylo)
    sibs = pl.ds(pl.multiple_of(((a * 4 + b) * 2 + ylo) * BLK, BLK), BLK)

    def local(src, dst, i):
        return pltpu.make_async_copy(src, dst, lsem.at[i])

    def opening(codes, scales):
        loads = [local(gc, codes.at[0], 0), local(gs, scales.at[0], 1), local(uc, codes.at[1], 2), local(us, scales.at[1], 3),
                 local(ds, scales.at[2], 4)]
        own_acts = local(acts.at[mine, :], A.at[own, 0:HALF], 5)
        own_cot = local(cot.at[mine, :], C.at[own, 0:HALF], 6)
        for load in (own_acts, loads[0], loads[1], own_cot, loads[2], loads[3], loads[4]):
            load.start()

        barrier = pltpu.get_barrier_semaphore()
        peers = [sib, lo, hi] + [apeer(d) for d in DELTAS] + [bpeer(d) for d in DELTAS]
        for peer in peers:
            pl.semaphore_signal(barrier, inc=1, device_id=peer, device_id_type=MESH)
        pl.semaphore_wait(barrier, len(peers))

        send(acts.at[theirs, :], A.at[sibs, HALF:WIDE], ACTS + SIB, ACTS + SIB, sib)
        send(cot.at[theirs, :], C.at[sibs, HALF:WIDE], COT + SIB, COT + SIB, sib)
        own_acts.wait()
        got(A.at[own, HALF:WIDE], ACTS + SIB, sib)
        send(A.at[own, :], A.at[own, :], ACTS + YLO, ACTS + YLO, lo)
        for d in DELTAS:
            send(A.at[own, :], A.at[own, :], ACTS + AOWN + d - 1, ACTS + AOWN + 3 - d, apeer(d))
        own_cot.wait()
        got(C.at[own, HALF:WIDE], COT + SIB, sib)
        send(C.at[own, :], C.at[own, :], COT + YLO, COT + YLO, lo)

        def dequantize(slot, which, w, first):
            def tile(i, _):
                r = pl.ds(pl.multiple_of(i * 32, 32), 32)
                rw = pl.ds(pl.multiple_of(first + i * 32, 32), 32)
                for g in range(HALF // GROUP):
                    cols = slice(g * GROUP, (g + 1) * GROUP)
                    w[rw, cols] = (codes[slot, r, cols].astype(F32) * scales[which, r, g:g + 1]).astype(BF16)
                return 0

            lax.fori_loop(0, HID // 32, tile, 0)

        down = local(dc, codes.at[0], 7)
        loads[0].wait()
        loads[1].wait()
        dequantize(0, 0, W2, 0)
        send(W2.at[0:HID, 0:HALF], W2.at[0:HID, HALF:WIDE], WTS, WTS, sib)
        down.start()
        loads[2].wait()
        loads[3].wait()
        dequantize(1, 1, W2, HID)
        send(W2.at[HID:2 * HID, 0:HALF], W2.at[HID:2 * HID, HALF:WIDE], WTS + 1, WTS + 1, sib)
        got(A.at[other, :], ACTS + YLO, lo)
        for d in DELTAS:
            send(A.at[other, :], A.at[other, :], ACTS + ALO + d - 1, ACTS + ALO + 3 - d, apeer(d))
        loads[4].wait()
        down.wait()
        dequantize(0, 2, WD, 0)
        send(WD.at[:, 0:HALF], WD.at[:, HALF:WIDE], WTS + 2, WTS + 2, sib)

    pl.run_scoped(opening, pltpu.VMEM((2, HID, HALF), jnp.int32), pltpu.VMEM((3, HID, HALF // GROUP), F32))

    def gate_up(k):
        block = A[rows(k), :]
        for part in range(2):
            r = slice(part * HID, (part + 1) * HID)
            TO[k, r, :] = nt(W2[r, :], block).astype(BF16)
        send(TO.at[k, 0:2 * HID, :], TR.at[k, 0:2 * HID, :], TFGU + k, TFGU + k, hi)

    def grad_hidden(k):
        TO[k, 2 * HID:3 * HID, :] = nt(WD[...], C[rows(k), :]).astype(BF16)

    def send_grad_hidden(k):
        send(TO.at[k, 2 * HID:3 * HID, :], TR.at[k, 2 * HID:3 * HID, :], TFGH + k, TFGH + k, hi)

    for d in DELTAS:
        got(A.at[blk((a + d) % 4, ylo), :], ACTS + AOWN + d - 1, apeer(d))
        got(A.at[blk((a + d) % 4, 1 - ylo), :], ACTS + ALO + d - 1, apeer(d))

    def bsend(buf, base, h, d):
        r = rows(chunk(b, h))
        send(buf.at[r, :], buf.at[r, :], base + BH + 3 * h + d - 1, base + BH + 3 * h + 3 - d, bpeer(d))

    def bgot(buf, base, h, d):
        got(buf.at[rows(chunk((b + d) % 4, h)), :], base + BH + 3 * h + d - 1, bpeer(d))

    for d in DELTAS:
        bsend(A, ACTS, 0, d)
    for part in range(2):
        got(W2.at[part * HID:(part + 1) * HID, HALF:WIDE], WTS + part, sib)

    def first(h, _):
        gate_up(chunk(b, h))
        return 0

    lax.fori_loop(0, 2, first, 0)

    def second(j, _):
        d = 1 + 2 * j - 3 * (j // 2)
        bgot(A, ACTS, 0, d)
        bsend(A, ACTS, 1, d)
        gate_up(chunk((b + d) % 4, 0))
        return 0

    lax.fori_loop(0, 3, second, 0)
    got(C.at[other, :], COT + YLO, lo)

    def third(j, _):
        d = 1 + 2 * j - 3 * (j // 2)
        bgot(A, ACTS, 1, d)
        send(C.at[pair(a), :], C.at[pair(a), :], COT + AOWN + d - 1, COT + AOWN + 3 - d, apeer(d))
        gate_up(chunk((b + d) % 4, 1))
        return 0

    lax.fori_loop(0, 3, third, 0)

    for part in range(2):
        sent(W2.at[part * HID:(part + 1) * HID, 0:HALF], WTS + part, sib)
    pl.semaphore_signal(credit, inc=1, device_id=sib, device_id_type=MESH)

    for d in DELTAS:
        got(C.at[pair((a + d) % 4), :], COT + AOWN + d - 1, apeer(d))
    for d in DELTAS:
        bsend(C, COT, 0, d)
    got(WD.at[:, HALF:WIDE], WTS + 2, sib)

    def activate(k):
        got(TR.at[k, 0:2 * HID, :], TFGU + k, hi)
        sent(TO.at[k, 0:2 * HID, :], TFGU + k, hi)

        def tile(i, _):
            r = pl.ds(pl.multiple_of(i * 32, 32), 32)
            q = pl.ds(pl.multiple_of(HID + i * 32, 32), 32)
            gate = TO[k, r, :].astype(F32) + TR[k, r, :].astype(F32)
            up = TO[k, q, :].astype(F32) + TR[k, q, :].astype(F32)
            s = 1.0 / (1.0 + jnp.exp(-gate))
            silu = gate * s
            TO[k, r, :] = (silu * up).astype(BF16)
            TR[k, r, :] = silu.astype(BF16)
            TR[k, q, :] = (up * (s * (1.0 + gate * (1.0 - s)))).astype(BF16)
            return 0

        lax.fori_loop(0, HID // 32, tile, 0)

    def transpose(k):
        HT[...] = jnp.transpose(TO[k, 0:HID, :].astype(F32)).astype(BF16)

    def output_part(h, d):
        k = chunk((b + d) % 4, h)
        activate(k)
        transpose(k)
        o = pl.ds(pl.multiple_of(((d - 1) * 2 + h) * CH, CH), CH)

        def tile(i, _):
            cols = pl.ds(pl.multiple_of(i * 512, 512), 512)
            O[o, cols] = nn(HT[...], WD[:, cols]).astype(BF16)
            return 0

        lax.fori_loop(0, WIDE // 512, tile, 0)
        to = pl.ds(pl.multiple_of(((3 - d) * 2 + h) * CH, CH), CH)
        send(O.at[o, :], RB.at[to, :], RSB + (d - 1) * 2 + h, RSB + (3 - d) * 2 + h, bpeer(d))

    def own_hidden(h, _):
        activate(chunk(b, h))
        return 0

    lax.fori_loop(0, 2, own_hidden, 0)

    def own_grad_hidden(h, _):
        grad_hidden(chunk(b, h))
        return 0

    lax.fori_loop(0, 2, own_grad_hidden, 0)

    def fourth(j, _):
        d = 1 + 2 * j - 3 * (j // 2)
        output_part(0, d)
        bgot(C, COT, 0, d)
        bsend(C, COT, 1, d)
        grad_hidden(chunk((b + d) % 4, 0))
        return 0

    lax.fori_loop(0, 3, fourth, 0)

    def fifth(j, _):
        d = 1 + 2 * j - 3 * (j // 2)
        output_part(1, d)
        bgot(C, COT, 1, d)
        grad_hidden(chunk((b + d) % 4, 1))
        send_grad_hidden(chunk(bd(j), 0))
        return 0

    lax.fori_loop(0, 3, fifth, 0)

    def sixth(j, _):
        send_grad_hidden(chunk(bd(j), 1))
        return 0

    lax.fori_loop(0, 3, sixth, 0)
    for h in range(2):
        send_grad_hidden(chunk(b, h))

    def closing(gsum, dsum):
        gsum[...] = jnp.zeros_like(gsum)
        dsum[...] = jnp.zeros_like(dsum)

        def down_step(k, _):
            def tile(i, _):
                cols = pl.ds(pl.multiple_of(i * 512, 512), 512)
                dsum[:, cols] += nn(TO[k, 0:HID, :], C[rows(k), cols])
                return 0

            return lax.fori_loop(0, WIDE // 512, tile, 0)

        lax.fori_loop(0, 8, down_step, 0)

        def narrow(i, _):
            r = pl.ds(pl.multiple_of(i * 32, 32), 32)
            DS[r, :] = dsum[r, HALF:WIDE].astype(BF16)
            return 0

        lax.fori_loop(0, HID // 32, narrow, 0)
        send(DS, DR, GRD, GRD, sib)

        def slopes(k):
            got(TR.at[k, 2 * HID:3 * HID, :], TFGH + k, hi)

            def tile(i, _):
                r = pl.ds(pl.multiple_of(i * 32, 32), 32)
                q = pl.ds(pl.multiple_of(HID + i * 32, 32), 32)
                w = pl.ds(pl.multiple_of(2 * HID + i * 32, 32), 32)
                grad = TO[k, w, :].astype(F32) + TR[k, w, :].astype(F32)
                TR[k, r, :] = (grad * TR[k, r, :].astype(F32)).astype(BF16)
                TR[k, q, :] = (grad * TR[k, q, :].astype(F32)).astype(BF16)
                return 0

            lax.fori_loop(0, HID // 32, tile, 0)

        def weigh(k, low, high):
            def tile(i, _):
                cols = pl.ds(pl.multiple_of(i * 256, 256), 256)
                gsum[:, cols] += nn(TR[k, 0:2 * HID, :], A[rows(k), cols])
                return 0

            lax.fori_loop(low, high, tile, 0)

        def gate_step(k):
            slopes(k)
            weigh(k, 0, WIDE // 256)

        def remote_step(j, h):
            gate_step(chunk(bd(j), h))

        lax.fori_loop(0, 3, lambda j, _: (remote_step(j, 0), 0)[1], 0)

        for d in DELTAS:
            for h in range(2):
                s = (d - 1) * 2 + h
                got(RB.at[s * CH:(s + 1) * CH, :], RSB + s, bpeer(d))

        def badd(h, _):
            transpose(chunk(b, h))
            r = [pl.ds(pl.multiple_of((2 * i + h) * CH, CH), CH) for i in range(3)]

            def tile(i, _):
                cols = pl.ds(pl.multiple_of(i * 256, 256), 256)
                total = nn(HT[...], WD[:, cols])
                for q in r:
                    total = total + RB[q, cols].astype(F32)
                RB[r[0], cols] = total.astype(BF16)
                return 0

            return lax.fori_loop(0, WIDE // 256, tile, 0)

        lax.fori_loop(0, 2, badd, 0)

        def part(a_):
            return pl.ds(pl.multiple_of(a_ * 2 * BLK, 2 * BLK), 2 * BLK)

        def slot(d):
            return pl.ds((d - 1) * 2 * BLK, 2 * BLK)

        for d in DELTAS:
            send(RB.at[part((a + d) % 4), :], RA.at[slot(4 - d), :], RSA + d - 1, RSA + 3 - d, apeer(d))
        lax.fori_loop(0, 2, lambda j, _: (remote_step(j, 1), 0)[1], 0)

        for d in DELTAS:
            got(RA.at[slot(d), :], RSA + d - 1, apeer(d))

        def aadd(i, _):
            cols = pl.ds(pl.multiple_of(i * 256, 256), 256)
            total = RB[part(a), cols].astype(F32)
            for d in DELTAS:
                total = total + RA[slot(d), cols].astype(F32)
            RB[part(a), cols] = total.astype(BF16)
            return 0

        lax.fori_loop(0, WIDE // 256, aadd, 0)

        def half(ylo_):
            return pl.ds(pl.multiple_of((a * 2 + ylo_) * BLK, BLK), BLK)

        send(RB.at[half(1 - ylo), :], RY, RSY, RSY, lo)
        remote_step(2, 1)
        gate_step(chunk(b, 0))

        got(RY, RSY, lo)
        RB[half(ylo), :] = (RB[half(ylo), :].astype(F32) + RY[...].astype(F32)).astype(BF16)
        send(RB.at[half(ylo), HALF:WIDE], out.at[mine, :], OUTS, OUTS, sib)
        keep = local(RB.at[half(ylo), 0:HALF], out.at[mine, :], 0)
        keep.start()

        got(DR, GRD, sib)

        def down_add(i, _):
            r = pl.ds(pl.multiple_of(i * 32, 32), 32)
            dsum[r, 0:HALF] += DR[r, :].astype(F32)
            return 0

        lax.fori_loop(0, HID // 32, down_add, 0)
        put_down = local(dsum.at[:, 0:HALF], gd, 1)
        put_down.start()

        last = chunk(b, 1)
        slopes(last)
        weigh(last, HALF // 256, WIDE // 256)
        pl.semaphore_wait(credit, 1)

        def narrow_gates(i, _):
            r = pl.ds(pl.multiple_of(i * 32, 32), 32)
            W2[r, 0:HALF] = gsum[r, HALF:WIDE].astype(BF16)
            return 0

        lax.fori_loop(0, 2 * HID // 32, narrow_gates, 0)
        send(W2.at[:, 0:HALF], W2.at[:, HALF:WIDE], GRU, GRU, sib)
        weigh(last, 0, HALF // 256)
        got(W2.at[:, HALF:WIDE], GRU, sib)

        def gates_add(i, _):
            r = pl.ds(pl.multiple_of(i * 32, 32), 32)
            gsum[r, 0:HALF] += W2[r, HALF:WIDE].astype(F32)
            return 0

        lax.fori_loop(0, 2 * HID // 32, gates_add, 0)
        put_up = local(gsum.at[0:HID, 0:HALF], gu, 2)
        put_gate = local(gsum.at[HID:2 * HID, 0:HALF], gg, 3)
        put_up.start()
        put_gate.start()

        sent(acts.at[theirs, :], ACTS + SIB, sib)
        sent(cot.at[theirs, :], COT + SIB, sib)
        sent(A.at[own, :], ACTS + YLO, lo)
        sent(C.at[own, :], COT + YLO, lo)
        for d in DELTAS:
            sent(A.at[own, :], ACTS + AOWN + d - 1, apeer(d))
            sent(A.at[other, :], ACTS + ALO + d - 1, apeer(d))
            sent(C.at[pair(a), :], COT + AOWN + d - 1, apeer(d))
            sent(RB.at[part((a + d) % 4), :], RSA + d - 1, apeer(d))
            for h in range(2):
                r = rows(chunk(b, h))
                sent(A.at[r, :], ACTS + BH + 3 * h + d - 1, bpeer(d))
                sent(C.at[r, :], COT + BH + 3 * h + d - 1, bpeer(d))
                s = (d - 1) * 2 + h
                sent(O.at[s * CH:(s + 1) * CH, :], RSB + s, bpeer(d))
        sent(WD.at[:, 0:HALF], WTS + 2, sib)
        for k in range(8):
            sent(TO.at[k, 2 * HID:3 * HID, :], TFGH + k, hi)
        sent(RB.at[half(1 - ylo), :], RSY, lo)
        sent(RB.at[half(ylo), HALF:WIDE], OUTS, sib)
        sent(DS, GRD, sib)
        sent(W2.at[:, 0:HALF], GRU, sib)
        got(out.at[theirs, :], OUTS, sib)
        keep.wait()
        put_down.wait()
        put_up.wait()
        put_gate.wait()

    pl.run_scoped(closing, pltpu.VMEM((2 * HID, WIDE), F32), pltpu.VMEM((HID, WIDE), F32))


def local_step(acts, gc, gs, uc, us, dc, ds, cot):
    anywhere = pl.BlockSpec(memory_space=pl.ANY)
    out, gg, gu, gd = pl.pallas_call(
        kernel,
        out_shape=(
            jax.ShapeDtypeStruct((2 * BLK, HALF), BF16),
            jax.ShapeDtypeStruct((HID, HALF), F32),
            jax.ShapeDtypeStruct((HID, HALF), F32),
            jax.ShapeDtypeStruct((HID, HALF), F32),
        ),
        in_specs=[anywhere] * 8,
        out_specs=(anywhere,) * 4,
        scratch_shapes=[
            pltpu.VMEM((8 * CH, WIDE), BF16),
            pltpu.VMEM((8 * CH, WIDE), BF16),
            pltpu.VMEM((2 * HID, WIDE), BF16),
            pltpu.VMEM((HID, WIDE), BF16),
            pltpu.VMEM((8, 3 * HID, CH), BF16),
            pltpu.VMEM((8, 3 * HID, CH), BF16),
            pltpu.VMEM((6 * CH, WIDE), BF16),
            pltpu.VMEM((6 * CH, WIDE), BF16),
            pltpu.VMEM((6 * BLK, WIDE), BF16),
            pltpu.VMEM((BLK, WIDE), BF16),
            pltpu.VMEM((CH, HID), BF16),
            pltpu.VMEM((HID, HALF), BF16),
            pltpu.VMEM((HID, HALF), BF16),
            pltpu.SemaphoreType.DMA((NSEM,)),
            pltpu.SemaphoreType.DMA((NSEM,)),
            pltpu.SemaphoreType.DMA((8,)),
            pltpu.SemaphoreType.REGULAR,
        ],
        compiler_params=pltpu.CompilerParams(collective_id=0, has_side_effects=True, vmem_limit_bytes=63 << 20),
        name="swiglu_step",
    )(acts, gc, gs, uc, us, dc, ds, cot)
    return out, gg, gu, gd


def solution(mesh):
    spec = P("fsdp", "tp")
    return jax.shard_map(local_step, mesh=mesh, in_specs=(spec,) * 8, out_specs=(spec,) * 4, check_vma=False)
```

```python
import functools

import jax
import jax.numpy as jnp
from jax import lax
from jax.experimental import pallas as pl
from jax.experimental.pallas import tpu as pltpu
from jax.sharding import PartitionSpec as P

MESH = pl.DeviceIdType.MESH
F32, BF16 = jnp.float32, jnp.bfloat16
GROUP = 128
HID = 448
HALF = 1024
WIDE = 2 * HALF
BLK = 64
CH = 256

ACTS, COT, WTS, TFGU, TFGH, RSB, RSA, RSY, OUTS, GRD, GRU, NSEM = 0, 26, 52, 55, 63, 71, 77, 83, 84, 85, 86, 87
SIB, YLO, AOWN, ALO, BPAIR = 0, 1, 2, 6, 10


def nt(left, right):
    return lax.dot_general(left, right, (((1,), (1,)), ((), ())), preferred_element_type=F32)


def nn(left, right):
    return lax.dot_general(left, right, (((1,), (0,)), ((), ())), preferred_element_type=F32)


def kernel(acts, gc, gs, uc, us, dc, ds, cot, out, gg, gu, gd,
           A, C, W2, WD, TO, TR, O, RB, RA, RY, HT, DS, DR, ssem, rsem, lsem, credit):
    f, t = lax.axis_index("fsdp"), lax.axis_index("tp")
    x, ylo, z = f % 4, (f // 4) % 2, f // 8
    yhi, c = t // 2, t % 2
    a = x * (1 - c) + z * c
    b = z * (1 - c) + x * c

    def dev(x_, ylo_, z_, yhi_, c_):
        return (z_ * 8 + ylo_ * 4 + x_, yhi_ * 2 + c_)

    def apeer(d):
        return dev((x + d * (1 - c)) % 4, ylo, (z + d * c) % 4, yhi, c)

    def bpeer(d):
        return dev((x + d * c) % 4, ylo, (z + d * (1 - c)) % 4, yhi, c)

    sib = dev(x, ylo, z, yhi, 1 - c)
    lo = dev(x, 1 - ylo, z, yhi, c)
    hi = dev(x, ylo, z, 1 - yhi, c)

    def rc(src, dst, s, r, to):
        return pltpu.make_async_remote_copy(src_ref=src, dst_ref=dst, send_sem=ssem.at[s], recv_sem=rsem.at[r],
                                            device_id=to, device_id_type=MESH)

    def send(src, dst, s, r, to):
        rc(src, dst, s, r, to).start()

    def got(dst, r, to):
        rc(dst, dst, 0, r, to).wait_recv()

    def sent(src, s, to):
        rc(src, src, s, 0, to).wait_send()

    def span(row, n):
        return pl.ds(pl.multiple_of(row, n), n)

    def blk(a_, ylo_):
        return span(((b * 4 + a_) * 2 + ylo_) * BLK, BLK)

    def chunk(d, h):
        return ((b + d) % 4) * 2 + (a // 2 + h) % 2

    def rows(k):
        return pl.ds(pl.multiple_of(k * CH, CH), CH)

    mine = pl.ds(pl.multiple_of(c * BLK, BLK), BLK)
    theirs = pl.ds(pl.multiple_of((1 - c) * BLK, BLK), BLK)
    own = blk(a, ylo)
    other = blk(a, 1 - ylo)
    sibs = pl.ds(pl.multiple_of(((a * 4 + b) * 2 + ylo) * BLK, BLK), BLK)

    def local(src, dst, i):
        return pltpu.make_async_copy(src, dst, lsem.at[i])

    class Round:
        def __init__(self, buf, row, n, base, peer):
            self.buf, self.row, self.n, self.base, self.peer = buf, row, n, base, peer

        def view(self, d, half=None):
            if half is None:
                return self.buf.at[span(self.row(d), self.n), :]
            return self.buf.at[span(self.row(d) + half * (self.n // 2), self.n // 2), :]

        def start(self):
            send(self.view(0), self.view(0), self.base, self.base + 1, self.peer(1))
            send(self.view(0), self.view(0), self.base + 1, self.base, self.peer(3))

        def forward(self):
            got(self.view(1), self.base, self.peer(1))
            send(self.view(1, 0), self.view(1, 0), self.base + 2, self.base + 2, self.peer(3))
            got(self.view(3), self.base + 1, self.peer(3))
            send(self.view(3, 1), self.view(3, 1), self.base + 3, self.base + 3, self.peer(1))

        def finish(self):
            got(self.view(2, 0), self.base + 2, self.peer(1))
            got(self.view(2, 1), self.base + 3, self.peer(3))

        def drain(self):
            sent(self.view(0), self.base, self.peer(1))
            sent(self.view(0), self.base + 1, self.peer(3))
            sent(self.view(1, 0), self.base + 2, self.peer(3))
            sent(self.view(3, 1), self.base + 3, self.peer(1))

    opposite = (a + 2) % 4
    order = (a, a + 1 - 2 * (a % 2), opposite + 1 - 2 * (opposite % 2), opposite)

    def rounds(buf, base):
        def around_a(ylo_, sem):
            return Round(buf, lambda d: ((b * 4 + (a + d) % 4) * 2 + ylo_) * BLK, BLK, base + sem, apeer)

        def around_b(i):
            return Round(buf, lambda d: (((b + d) % 4) * 4 + order[i]) * 2 * BLK, 2 * BLK, base + BPAIR + 4 * i, bpeer)

        return [around_a(ylo, AOWN), around_a(1 - ylo, ALO)], [around_b(i) for i in range(4)]

    acts_a, acts_b = rounds(A, ACTS)
    cot_a, cot_b = rounds(C, COT)

    def opening(codes, scales, turned):
        loads = [local(gc, codes.at[0], 0), local(gs, turned.at[0], 1), local(uc, codes.at[1], 2), local(us, turned.at[1], 3),
                 local(ds, turned.at[2], 4)]
        own_acts = local(acts.at[mine, :], A.at[own, 0:HALF], 5)
        own_cot = local(cot.at[mine, :], C.at[own, 0:HALF], 6)
        for load in (own_acts, loads[0], loads[1], own_cot, loads[2], loads[3], loads[4]):
            load.start()

        barrier = pltpu.get_barrier_semaphore()
        peers = [sib, lo, hi, apeer(1), apeer(3), bpeer(1), bpeer(3)]
        for peer in peers:
            pl.semaphore_signal(barrier, inc=1, device_id=peer, device_id_type=MESH)
        pl.semaphore_wait(barrier, len(peers))

        send(acts.at[theirs, :], A.at[sibs, HALF:WIDE], ACTS + SIB, ACTS + SIB, sib)
        send(cot.at[theirs, :], C.at[sibs, HALF:WIDE], COT + SIB, COT + SIB, sib)
        own_acts.wait()
        got(A.at[own, HALF:WIDE], ACTS + SIB, sib)
        send(A.at[own, :], A.at[own, :], ACTS + YLO, ACTS + YLO, lo)
        acts_a[0].start()
        own_cot.wait()
        got(C.at[own, HALF:WIDE], COT + SIB, sib)
        send(C.at[own, :], C.at[own, :], COT + YLO, COT + YLO, lo)
        cot_a[0].start()

        def dequantize(slot, which, w, first):
            scales[which] = jnp.transpose(turned[which])

            def tile(i, _):
                r = span(i * 32, 32)
                rw = span(first + i * 32, 32)
                for g in range(HALF // GROUP):
                    cols = slice(g * GROUP, (g + 1) * GROUP)
                    w[rw, cols] = (codes[slot, r, cols].astype(F32) * scales[which, r, g:g + 1]).astype(BF16)
                return 0

            lax.fori_loop(0, HID // 32, tile, 0)

        down = local(dc, codes.at[0], 7)
        loads[0].wait()
        loads[1].wait()
        dequantize(0, 0, W2, 0)
        send(W2.at[0:HID, 0:HALF], W2.at[0:HID, HALF:WIDE], WTS, WTS, sib)
        down.start()
        acts_a[0].forward()
        loads[2].wait()
        loads[3].wait()
        dequantize(1, 1, W2, HID)
        send(W2.at[HID:2 * HID, 0:HALF], W2.at[HID:2 * HID, HALF:WIDE], WTS + 1, WTS + 1, sib)
        got(A.at[other, :], ACTS + YLO, lo)
        acts_a[1].start()
        acts_b[0].start()
        loads[4].wait()
        down.wait()
        dequantize(0, 2, WD, 0)
        send(WD.at[:, 0:HALF], WD.at[:, HALF:WIDE], WTS + 2, WTS + 2, sib)

    pl.run_scoped(opening, pltpu.VMEM((2, HID, HALF), jnp.int32), pltpu.VMEM((3, HID, HALF // GROUP), F32),
                  pltpu.VMEM((3, HALF // GROUP, HID), F32))

    def gate_up(k):
        block = A[rows(k), :]
        for part in range(2):
            r = slice(part * HID, (part + 1) * HID)
            TO[k, r, :] = nt(W2[r, :], block).astype(BF16)
        send(TO.at[k, 0:2 * HID, :], TR.at[k, 0:2 * HID, :], TFGU + k, TFGU + k, hi)

    def grad_hidden(k):
        TO[k, 2 * HID:3 * HID, :] = nt(WD[...], C[rows(k), :]).astype(BF16)

    def send_grad_hidden(k):
        send(TO.at[k, 2 * HID:3 * HID, :], TR.at[k, 2 * HID:3 * HID, :], TFGH + k, TFGH + k, hi)

    def activate(k):
        got(TR.at[k, 0:2 * HID, :], TFGU + k, hi)
        sent(TO.at[k, 0:2 * HID, :], TFGU + k, hi)

        def tile(i, _):
            r, q = span(i * 32, 32), span(HID + i * 32, 32)
            gate = TO[k, r, :].astype(F32) + TR[k, r, :].astype(F32)
            up = TO[k, q, :].astype(F32) + TR[k, q, :].astype(F32)
            s = 1.0 / (1.0 + jnp.exp(-gate))
            silu = gate * s
            TO[k, r, :] = (silu * up).astype(BF16)
            TR[k, r, :] = silu.astype(BF16)
            TR[k, q, :] = (up * (s * (1.0 + gate * (1.0 - s)))).astype(BF16)
            return 0

        lax.fori_loop(0, HID // 32, tile, 0)

    def transpose(k):
        HT[...] = jnp.transpose(TO[k, 0:HID, :].astype(F32)).astype(BF16)

    def oslot(d, h):
        return span(((d - 1) * 2 + h) * CH, CH)

    def rslot(i):
        return span(i * CH, CH)

    def output_part(d, h):
        k = chunk(d, h)
        activate(k)
        transpose(k)
        o = oslot(d, h)

        def tile(i, _):
            cols = span(i * 512, 512)
            O[o, cols] = nn(HT[...], WD[:, cols]).astype(BF16)
            return 0

        lax.fori_loop(0, WIDE // 512, tile, 0)

    def loop(n, body):
        lax.fori_loop(0, n, lambda i, _: (body(i), 0)[1], 0)

    acts_a[1].forward()
    acts_b[1].start()
    acts_b[2].start()
    for part in range(2):
        got(W2.at[part * HID:(part + 1) * HID, HALF:WIDE], WTS + part, sib)
    gate_up(chunk(0, 0))
    acts_a[0].finish()
    acts_a[1].finish()
    acts_b[3].start()
    gate_up(chunk(0, 1))
    cot_a[0].forward()
    got(C.at[other, :], COT + YLO, lo)
    cot_a[1].start()
    acts_b[0].forward()
    acts_b[1].forward()
    loop(2, lambda j: gate_up(chunk(1 + 2 * j, 0)))
    cot_a[1].forward()
    acts_b[2].forward()
    acts_b[3].forward()
    cot_a[0].finish()
    cot_a[1].finish()
    for r in cot_b:
        r.start()
    loop(2, lambda j: gate_up(chunk(1 + 2 * j, 1)))
    loop(2, lambda h: activate(chunk(0, h)))
    acts_b[0].finish()
    acts_b[1].finish()
    gate_up(chunk(2, 0))
    acts_b[2].finish()
    acts_b[3].finish()
    gate_up(chunk(2, 1))

    for part in range(2):
        sent(W2.at[part * HID:(part + 1) * HID, 0:HALF], WTS + part, sib)
    pl.semaphore_signal(credit, inc=1, device_id=sib, device_id_type=MESH)

    got(WD.at[:, HALF:WIDE], WTS + 2, sib)
    output_part(1, 0)
    cot_b[0].forward()
    cot_b[1].forward()
    loop(2, lambda h: grad_hidden(chunk(0, h)))
    output_part(3, 0)
    send(O.at[oslot(3, 0), :], RB.at[rslot(4), :], RSB + 4, RSB + 4, bpeer(3))
    cot_b[2].forward()
    cot_b[3].forward()
    loop(2, lambda j: grad_hidden(chunk(1 + 2 * j, 0)))
    output_part(1, 1)
    send(O.at[oslot(1, 1), :], RB.at[rslot(3), :], RSB + 3, RSB + 3, bpeer(1))
    loop(2, lambda j: grad_hidden(chunk(1 + 2 * j, 1)))
    output_part(3, 1)
    output_part(2, 0)
    send(O.at[oslot(2, 0), :], RB.at[rslot(0), :], RSB, RSB, bpeer(1))
    loop(2, lambda h: send_grad_hidden(chunk(0, h)))
    output_part(2, 1)
    send(O.at[oslot(2, 1), :], RB.at[rslot(1), :], RSB + 1, RSB + 1, bpeer(3))
    loop(2, lambda j: send_grad_hidden(chunk(1 + 2 * j, 0)))
    loop(2, lambda j: send_grad_hidden(chunk(1 + 2 * j, 1)))
    cot_b[0].finish()
    cot_b[1].finish()
    grad_hidden(chunk(2, 0))
    send_grad_hidden(chunk(2, 0))
    cot_b[2].finish()
    cot_b[3].finish()
    grad_hidden(chunk(2, 1))
    send_grad_hidden(chunk(2, 1))

    def closing(gsum, dsum):
        def down_step(k, _):
            def tile(i):
                cols = span(i * 512, 512)
                dsum[:, cols] += nn(TO[k, 0:HID, :], C[rows(k), cols])

            loop(WIDE // 512, tile)
            return 0

        def slopes(k):
            got(TR.at[k, 2 * HID:3 * HID, :], TFGH + k, hi)

            def tile(i):
                r, q, w = span(i * 32, 32), span(HID + i * 32, 32), span(2 * HID + i * 32, 32)
                grad = TO[k, w, :].astype(F32) + TR[k, w, :].astype(F32)
                TR[k, r, :] = (grad * TR[k, r, :].astype(F32)).astype(BF16)
                TR[k, q, :] = (grad * TR[k, q, :].astype(F32)).astype(BF16)

            loop(HID // 32, tile)

        def weigh(k, low, high):
            def tile(i, _):
                cols = span(i * 256, 256)
                gsum[:, cols] += nn(TR[k, 0:2 * HID, :], A[rows(k), cols])
                return 0

            lax.fori_loop(low, high, tile, 0)

        def gate_step(k):
            slopes(k)
            weigh(k, 0, WIDE // 256)

        gsum[...] = jnp.zeros_like(gsum)
        dsum[...] = jnp.zeros_like(dsum)
        lax.fori_loop(0, 8, down_step, 0)

        def narrow(i):
            r = span(i * 32, 32)
            DS[r, :] = dsum[r, HALF:WIDE].astype(BF16)

        loop(HID // 32, narrow)
        send(DS, DR, GRD, GRD, sib)

        loop(2, lambda h: gate_step(chunk(0, h)))

        def add_share(buf, r, other_buf, q):
            def tile(i):
                cols = span(i * 512, 512)
                buf[r, cols] = (buf[r, cols].astype(F32) + other_buf[q, cols].astype(F32)).astype(BF16)

            loop(WIDE // 512, tile)

        got(RB.at[rslot(0), :], RSB, bpeer(3))
        add_share(O, oslot(1, 0), RB, rslot(0))
        send(O.at[oslot(1, 0), :], RB.at[rslot(2), :], RSB + 2, RSB + 2, bpeer(1))
        got(RB.at[rslot(1), :], RSB + 1, bpeer(1))
        add_share(O, oslot(3, 1), RB, rslot(1))
        send(O.at[oslot(3, 1), :], RB.at[rslot(5), :], RSB + 5, RSB + 5, bpeer(3))

        loop(2, lambda j: gate_step(chunk(1 + 2 * j, 0)))

        got(RB.at[rslot(3), :], RSB + 3, bpeer(3))
        got(RB.at[rslot(4), :], RSB + 4, bpeer(1))
        got(RB.at[rslot(2), :], RSB + 2, bpeer(3))
        got(RB.at[rslot(5), :], RSB + 5, bpeer(1))

        def badd(h):
            transpose(chunk(0, h))
            q, w = rslot(2 + h), rslot(4 + h)

            def tile(i):
                cols = span(i * 256, 256)
                total = nn(HT[...], WD[:, cols]) + RB[q, cols].astype(F32) + RB[w, cols].astype(F32)
                RB[q, cols] = total.astype(BF16)

            loop(WIDE // 256, tile)

        loop(2, badd)

        def part(d, y):
            a_ = (a + d) % 4
            return span(2 * CH + ((a_ // 2 + a // 2) % 2) * CH + (a_ % 2) * 2 * BLK + y * BLK, BLK)

        def slot(i):
            return span(i * BLK, BLK)

        send(RB.at[part(2, 0), :], RA.at[slot(0), :], RSA, RSA, apeer(1))
        send(RB.at[part(2, 1), :], RA.at[slot(1), :], RSA + 1, RSA + 1, apeer(3))
        send(RB.at[part(1, 1), :], RA.at[slot(3), :], RSA + 3, RSA + 3, apeer(1))
        send(RB.at[part(3, 0), :], RA.at[slot(4), :], RSA + 4, RSA + 4, apeer(3))
        gate_step(chunk(1, 1))
        got(RA.at[slot(0), :], RSA, apeer(3))
        add_share(RB, part(1, 0), RA, slot(0))
        send(RB.at[part(1, 0), :], RA.at[slot(2), :], RSA + 2, RSA + 2, apeer(1))
        got(RA.at[slot(1), :], RSA + 1, apeer(1))
        add_share(RB, part(3, 1), RA, slot(1))
        send(RB.at[part(3, 1), :], RA.at[slot(5), :], RSA + 5, RSA + 5, apeer(3))
        gate_step(chunk(3, 1))
        got(RA.at[slot(3), :], RSA + 3, apeer(3))
        got(RA.at[slot(4), :], RSA + 4, apeer(1))
        got(RA.at[slot(2), :], RSA + 2, apeer(3))
        got(RA.at[slot(5), :], RSA + 5, apeer(1))

        def aadd(y):
            def tile(i):
                cols = span(i * 512, 512)
                total = RB[part(0, y), cols].astype(F32) + RA[slot(2 + y), cols].astype(F32) + RA[slot(4 + y), cols].astype(F32)
                RB[part(0, y), cols] = total.astype(BF16)

            loop(WIDE // 512, tile)

        aadd(1 - ylo)
        send(RB.at[part(0, 1 - ylo), :], RY, RSY, RSY, lo)
        aadd(ylo)
        got(DR, GRD, sib)

        def down_add(i):
            r = span(i * 32, 32)
            dsum[r, 0:HALF] += DR[r, :].astype(F32)

        loop(HID // 32, down_add)
        put_down = local(dsum.at[:, 0:HALF], gd, 1)
        put_down.start()
        gate_step(chunk(2, 0))

        last = chunk(2, 1)
        slopes(last)
        weigh(last, HALF // 256, WIDE // 256)
        pl.semaphore_wait(credit, 1)

        def narrow_gates(i):
            r = span(i * 32, 32)
            W2[r, 0:HALF] = gsum[r, HALF:WIDE].astype(BF16)

        loop(2 * HID // 32, narrow_gates)
        send(W2.at[:, 0:HALF], W2.at[:, HALF:WIDE], GRU, GRU, sib)
        weigh(last, 0, HALF // 256)

        got(RY, RSY, lo)
        add_share(RB, part(0, ylo), RY, pl.ds(0, BLK))
        send(RB.at[part(0, ylo), HALF:WIDE], out.at[mine, :], OUTS, OUTS, sib)
        keep = local(RB.at[part(0, ylo), 0:HALF], out.at[mine, :], 0)
        keep.start()
        got(W2.at[:, HALF:WIDE], GRU, sib)

        def gates_add(i):
            r = span(i * 32, 32)
            gsum[r, 0:HALF] += W2[r, HALF:WIDE].astype(F32)

        loop(2 * HID // 32, gates_add)
        put_up = local(gsum.at[0:HID, 0:HALF], gu, 2)
        put_gate = local(gsum.at[HID:2 * HID, 0:HALF], gg, 3)
        put_up.start()
        put_gate.start()

        sent(acts.at[theirs, :], ACTS + SIB, sib)
        sent(cot.at[theirs, :], COT + SIB, sib)
        sent(A.at[own, :], ACTS + YLO, lo)
        sent(C.at[own, :], COT + YLO, lo)
        for r in acts_a + acts_b + cot_a + cot_b:
            r.drain()
        sent(WD.at[:, 0:HALF], WTS + 2, sib)
        for k in range(8):
            sent(TO.at[k, 2 * HID:3 * HID, :], TFGH + k, hi)
        for i in range(6):
            sent(O.at[rslot(i), :], RSB + i, bpeer(1))
            sent(RA.at[slot(i), :], RSA + i, apeer(1))
        sent(RY, RSY, lo)
        sent(RB.at[part(0, ylo), HALF:WIDE], OUTS, sib)
        sent(DS, GRD, sib)
        sent(W2.at[:, 0:HALF], GRU, sib)
        got(out.at[theirs, :], OUTS, sib)
        keep.wait()
        put_down.wait()
        put_up.wait()
        put_gate.wait()

    pl.run_scoped(closing, pltpu.VMEM((2 * HID, WIDE), F32), pltpu.VMEM((HID, WIDE), F32))


def hand_over(*refs):
    kept, results, held, sems = refs[0:4], refs[4:8], refs[8:12], refs[12]
    pieces = [(i, j) for i in (1, 2, 3, 0) for j in range(1 if i == 0 else 2)]
    way_in, way_out = [], []
    for n, (i, j) in enumerate(pieces):
        r = pl.ds(0, 2 * BLK) if i == 0 else pl.ds(j * HID // 2, HID // 2)
        way_in.append(pltpu.make_async_copy(kept[i].at[r, :], held[i].at[r, :], sems.at[n]))
        way_out.append(pltpu.make_async_copy(held[i].at[r, :], results[i].at[r, :], sems.at[len(pieces) + n]))
    for copy in way_in:
        copy.start()
    for before, after in zip(way_in, way_out):
        before.wait()
        after.start()
    for copy in way_out:
        copy.wait()


def local_step(acts, gc, gs, uc, us, dc, ds, cot):
    anywhere = pl.BlockSpec(memory_space=pl.ANY)
    results = pl.pallas_call(
        kernel,
        out_shape=(
            jax.ShapeDtypeStruct((2 * BLK, HALF), BF16),
            jax.ShapeDtypeStruct((HID, HALF), F32),
            jax.ShapeDtypeStruct((HID, HALF), F32),
            jax.ShapeDtypeStruct((HID, HALF), F32),
        ),
        in_specs=[anywhere] * 8,
        out_specs=(anywhere,) * 4,
        scratch_shapes=[
            pltpu.VMEM((8 * CH, WIDE), BF16),
            pltpu.VMEM((8 * CH, WIDE), BF16),
            pltpu.VMEM((2 * HID, WIDE), BF16),
            pltpu.VMEM((HID, WIDE), BF16),
            pltpu.VMEM((8, 3 * HID, CH), BF16),
            pltpu.VMEM((8, 3 * HID, CH), BF16),
            pltpu.VMEM((6 * CH, WIDE), BF16),
            pltpu.VMEM((6 * CH, WIDE), BF16),
            pltpu.VMEM((6 * BLK, WIDE), BF16),
            pltpu.VMEM((BLK, WIDE), BF16),
            pltpu.VMEM((CH, HID), BF16),
            pltpu.VMEM((HID, HALF), BF16),
            pltpu.VMEM((HID, HALF), BF16),
            pltpu.SemaphoreType.DMA((NSEM,)),
            pltpu.SemaphoreType.DMA((NSEM,)),
            pltpu.SemaphoreType.DMA((8,)),
            pltpu.SemaphoreType.REGULAR,
        ],
        compiler_params=pltpu.CompilerParams(collective_id=0, has_side_effects=True, vmem_limit_bytes=63 << 20),
        name="swiglu_step",
    )(acts, gc, gs.T, uc, us.T, dc, ds.T, cot)
    return pl.pallas_call(
        hand_over,
        out_shape=tuple(jax.ShapeDtypeStruct(r.shape, r.dtype) for r in results),
        in_specs=[anywhere] * 4,
        out_specs=(anywhere,) * 4,
        scratch_shapes=[pltpu.VMEM(r.shape, r.dtype) for r in results] + [pltpu.SemaphoreType.DMA((14,))],
        compiler_params=pltpu.CompilerParams(vmem_limit_bytes=60 << 20),
        name="hand_over",
    )(*results)


def solution(mesh):
    spec = P("fsdp", "tp")
    return jax.shard_map(local_step, mesh=mesh, in_specs=(spec,) * 8, out_specs=(spec,) * 4, check_vma=False)
```

```python
import functools

import jax
import jax.numpy as jnp
from jax import lax
from jax.experimental import pallas as pl
from jax.experimental.pallas import tpu as pltpu
from jax.sharding import PartitionSpec as P

MESH = pl.DeviceIdType.MESH
F32, BF16 = jnp.float32, jnp.bfloat16
GROUP = 128
HID = 448
HALF = 1024
WIDE = 2 * HALF
BLK = 64
CH = 256

ACTS, COT, WTS, TFGU, TFGH, RSB, RSA, RSY, OUTS, GRD, GRU, PAIRS, NSEM = 0, 27, 54, 57, 65, 73, 79, 85, 86, 87, 88, 92, 94
SIB, YLO, YSIB, AOWN, ALO, BPAIR = 0, 1, 2, 3, 7, 11


def nt(left, right):
    return lax.dot_general(left, right, (((1,), (1,)), ((), ())), preferred_element_type=F32)


def nn(left, right):
    return lax.dot_general(left, right, (((1,), (0,)), ((), ())), preferred_element_type=F32)


def kernel(acts, gc, gs, uc, us, dc, ds, cot, out, gg, gu, gd,
           A, C, W2, WD, TO, TR, O, RB, RA, RY, HT, DS, DR, ssem, rsem, lsem, credit):
    f, t = lax.axis_index("fsdp"), lax.axis_index("tp")
    x, ylo, z = f % 4, (f // 4) % 2, f // 8
    yhi, c = t // 2, t % 2
    a = x * (1 - c) + z * c
    b = z * (1 - c) + x * c

    def dev(x_, ylo_, z_, yhi_, c_):
        return (z_ * 8 + ylo_ * 4 + x_, yhi_ * 2 + c_)

    def apeer(d):
        return dev((x + d * (1 - c)) % 4, ylo, (z + d * c) % 4, yhi, c)

    def bpeer(d):
        return dev((x + d * c) % 4, ylo, (z + d * (1 - c)) % 4, yhi, c)

    sib = dev(x, ylo, z, yhi, 1 - c)
    lo = dev(x, 1 - ylo, z, yhi, c)
    losib = dev(x, 1 - ylo, z, yhi, 1 - c)
    hi = dev(x, ylo, z, 1 - yhi, c)

    def rc(src, dst, s, r, to):
        return pltpu.make_async_remote_copy(src_ref=src, dst_ref=dst, send_sem=ssem.at[s], recv_sem=rsem.at[r],
                                            device_id=to, device_id_type=MESH)

    def send(src, dst, s, r, to):
        rc(src, dst, s, r, to).start()

    def got(dst, r, to):
        rc(dst, dst, 0, r, to).wait_recv()

    def sent(src, s, to):
        rc(src, src, s, 0, to).wait_send()

    def span(row, n):
        return pl.ds(pl.multiple_of(row, n), n)

    def blk(a_, ylo_):
        return span(((b * 4 + a_) * 2 + ylo_) * BLK, BLK)

    def chunk(d, h):
        return ((b + d) % 4) * 2 + (a // 2 + h) % 2

    def rows(k):
        return pl.ds(pl.multiple_of(k * CH, CH), CH)

    mine = pl.ds(pl.multiple_of(c * BLK, BLK), BLK)
    theirs = pl.ds(pl.multiple_of((1 - c) * BLK, BLK), BLK)
    own = blk(a, ylo)
    other = blk(a, 1 - ylo)
    sibs = pl.ds(pl.multiple_of(((a * 4 + b) * 2 + ylo) * BLK, BLK), BLK)

    def local(src, dst, i):
        return pltpu.make_async_copy(src, dst, lsem.at[i])

    class Round:
        def __init__(self, buf, row, n, base, peer):
            self.buf, self.row, self.n, self.base, self.peer = buf, row, n, base, peer

        def view(self, d, half=None):
            if half is None:
                return self.buf.at[span(self.row(d), self.n), :]
            return self.buf.at[span(self.row(d) + half * (self.n // 2), self.n // 2), :]

        def start(self):
            send(self.view(0), self.view(0), self.base, self.base + 1, self.peer(1))
            send(self.view(0), self.view(0), self.base + 1, self.base, self.peer(3))

        def forward(self):
            got(self.view(1), self.base, self.peer(1))
            send(self.view(1, 0), self.view(1, 0), self.base + 2, self.base + 2, self.peer(3))
            got(self.view(3), self.base + 1, self.peer(3))
            send(self.view(3, 1), self.view(3, 1), self.base + 3, self.base + 3, self.peer(1))

        def finish(self):
            got(self.view(2, 0), self.base + 2, self.peer(1))
            got(self.view(2, 1), self.base + 3, self.peer(3))

        def drain(self):
            sent(self.view(0), self.base, self.peer(1))
            sent(self.view(0), self.base + 1, self.peer(3))
            sent(self.view(1, 0), self.base + 2, self.peer(3))
            sent(self.view(3, 1), self.base + 3, self.peer(1))

    opposite = (a + 2) % 4
    order = (a, a + 1 - 2 * (a % 2), opposite + 1 - 2 * (opposite % 2), opposite)

    def rounds(buf, base):
        def around_a(ylo_, sem):
            return Round(buf, lambda d: ((b * 4 + (a + d) % 4) * 2 + ylo_) * BLK, BLK, base + sem, apeer)

        def around_b(i):
            return Round(buf, lambda d: (((b + d) % 4) * 4 + order[i]) * 2 * BLK, 2 * BLK, base + BPAIR + 4 * i, bpeer)

        return [around_a(ylo, AOWN), around_a(1 - ylo, ALO)], [around_b(i) for i in range(4)]

    acts_a, acts_b = rounds(A, ACTS)
    cot_a, cot_b = rounds(C, COT)

    def got_other(buf, base):
        got(buf.at[other, 0:HALF], base + YLO, lo)
        got(buf.at[other, HALF:WIDE], base + YSIB, losib)

    def opening(codes, scales, turned):
        loads = [local(gc, codes.at[0], 0), local(gs, turned.at[0], 1), local(uc, codes.at[1], 2), local(us, turned.at[1], 3),
                 local(ds, turned.at[2], 4)]
        own_acts = local(acts.at[mine, :], A.at[own, 0:HALF], 5)
        own_cot = local(cot.at[mine, :], C.at[own, 0:HALF], 6)
        for load in (own_acts, loads[0], loads[1], own_cot, loads[2], loads[3], loads[4]):
            load.start()

        barrier = pltpu.get_barrier_semaphore()
        peers = [sib, lo, losib, hi, apeer(1), apeer(3), bpeer(1), bpeer(3)]
        for peer in peers:
            pl.semaphore_signal(barrier, inc=1, device_id=peer, device_id_type=MESH)
        pl.semaphore_wait(barrier, len(peers))

        for x_, buf, base in ((acts, A, ACTS), (cot, C, COT)):
            send(x_.at[theirs, :], buf.at[sibs, HALF:WIDE], base + SIB, base + SIB, sib)
            send(x_.at[mine, :], buf.at[own, 0:HALF], base + YLO, base + YLO, lo)
            send(x_.at[theirs, :], buf.at[sibs, HALF:WIDE], base + YSIB, base + YSIB, losib)
        own_acts.wait()
        got(A.at[own, HALF:WIDE], ACTS + SIB, sib)
        acts_a[0].start()
        own_cot.wait()
        got(C.at[own, HALF:WIDE], COT + SIB, sib)
        cot_a[0].start()

        def dequantize(slot, which, w, first):
            scales[which] = jnp.transpose(turned[which])

            def tile(i, _):
                r = span(i * 32, 32)
                rw = span(first + i * 32, 32)
                for g in range(HALF // GROUP):
                    cols = slice(g * GROUP, (g + 1) * GROUP)
                    w[rw, cols] = (codes[slot, r, cols].astype(F32) * scales[which, r, g:g + 1]).astype(BF16)
                return 0

            lax.fori_loop(0, HID // 32, tile, 0)

        down = local(dc, codes.at[0], 7)
        loads[0].wait()
        loads[1].wait()
        dequantize(0, 0, W2, 0)
        send(W2.at[0:HID, 0:HALF], W2.at[0:HID, HALF:WIDE], WTS, WTS, sib)
        down.start()
        acts_a[0].forward()
        loads[2].wait()
        loads[3].wait()
        dequantize(1, 1, W2, HID)
        send(W2.at[HID:2 * HID, 0:HALF], W2.at[HID:2 * HID, HALF:WIDE], WTS + 1, WTS + 1, sib)
        got_other(A, ACTS)
        acts_a[1].start()
        acts_b[0].start()
        for part in range(2):
            got(W2.at[part * HID:(part + 1) * HID, HALF:WIDE], WTS + part, sib)
        gate_up_pair(0)
        loads[4].wait()
        down.wait()
        dequantize(0, 2, WD, 0)
        send(WD.at[:, 0:HALF], WD.at[:, HALF:WIDE], WTS + 2, WTS + 2, sib)

    def gate_up(k):
        block = A[rows(k), :]
        for part in range(2):
            r = slice(part * HID, (part + 1) * HID)
            TO[k, r, :] = nt(W2[r, :], block).astype(BF16)
        send(TO.at[k, 0:2 * HID, :], TR.at[k, 0:2 * HID, :], TFGU + k, TFGU + k, hi)

    def pair_cols(i):
        return span(((order[i] % 2) * 2 * BLK), 2 * BLK)

    def gate_up_pair(i):
        k, cols = chunk(0, 0), pair_cols(i)
        block = A[span((b * 4 + order[i]) * 2 * BLK, 2 * BLK), :]
        for part in range(2):
            r = slice(part * HID, (part + 1) * HID)
            TO[k, r, cols] = nt(W2[r, :], block).astype(BF16)
        send(TO.at[k, 0:2 * HID, cols], TR.at[k, 0:2 * HID, cols], PAIRS + i, PAIRS + i, hi)

    pl.run_scoped(opening, pltpu.VMEM((2, HID, HALF), jnp.int32), pltpu.VMEM((3, HID, HALF // GROUP), F32),
                  pltpu.VMEM((3, HALF // GROUP, HID), F32))

    def grad_hidden(k):
        TO[k, 2 * HID:3 * HID, :] = nt(WD[...], C[rows(k), :]).astype(BF16)

    def send_grad_hidden(k):
        send(TO.at[k, 2 * HID:3 * HID, :], TR.at[k, 2 * HID:3 * HID, :], TFGH + k, TFGH + k, hi)

    def hidden_share(k):
        grad_hidden(k)
        send_grad_hidden(k)

    def activate(k, pairs=False):
        if pairs:
            for i in range(2):
                got(TR.at[k, 0:2 * HID, pair_cols(i)], PAIRS + i, hi)
                sent(TO.at[k, 0:2 * HID, pair_cols(i)], PAIRS + i, hi)
        else:
            got(TR.at[k, 0:2 * HID, :], TFGU + k, hi)
            sent(TO.at[k, 0:2 * HID, :], TFGU + k, hi)

        def tile(i, _):
            r, q = span(i * 32, 32), span(HID + i * 32, 32)
            gate = TO[k, r, :].astype(F32) + TR[k, r, :].astype(F32)
            up = TO[k, q, :].astype(F32) + TR[k, q, :].astype(F32)
            s = 1.0 / (1.0 + jnp.exp(-gate))
            silu = gate * s
            TO[k, r, :] = (silu * up).astype(BF16)
            TR[k, r, :] = silu.astype(BF16)
            TR[k, q, :] = (up * (s * (1.0 + gate * (1.0 - s)))).astype(BF16)
            return 0

        lax.fori_loop(0, HID // 32, tile, 0)

    def transpose(k):
        HT[...] = jnp.transpose(TO[k, 0:HID, :].astype(F32)).astype(BF16)

    def oslot(d, h):
        return span(((d - 1) * 2 + h) * CH, CH)

    def rslot(i):
        return span(i * CH, CH)

    def output_part(d, h):
        k = chunk(d, h)
        activate(k)
        transpose(k)
        o = oslot(d, h)

        def tile(i, _):
            cols = span(i * 512, 512)
            O[o, cols] = nn(HT[...], WD[:, cols]).astype(BF16)
            return 0

        lax.fori_loop(0, WIDE // 512, tile, 0)

    def loop(n, body):
        lax.fori_loop(0, n, lambda i, _: (body(i), 0)[1], 0)

    def middle(gsum, dsum):
        def down_step(k):
            def tile(i):
                cols = span(i * 512, 512)
                dsum[:, cols] += nn(TO[k, 0:HID, :], C[rows(k), cols])

            loop(WIDE // 512, tile)

        def slopes(k):
            got(TR.at[k, 2 * HID:3 * HID, :], TFGH + k, hi)

            def tile(i):
                r, q, w = span(i * 32, 32), span(HID + i * 32, 32), span(2 * HID + i * 32, 32)
                grad = TO[k, w, :].astype(F32) + TR[k, w, :].astype(F32)
                TR[k, r, :] = (grad * TR[k, r, :].astype(F32)).astype(BF16)
                TR[k, q, :] = (grad * TR[k, q, :].astype(F32)).astype(BF16)

            loop(HID // 32, tile)

        def weigh(k, cols):
            gsum[:, cols] += nn(TR[k, 0:2 * HID, :], A[rows(k), cols])

        def gate_step(k):
            slopes(k)
            loop(WIDE // 256, lambda i: weigh(k, span(i * 256, 256)))

        def add_share(buf, r, other_buf, q):
            def tile(i):
                cols = span(i * 512, 512)
                buf[r, cols] = (buf[r, cols].astype(F32) + other_buf[q, cols].astype(F32)).astype(BF16)

            loop(WIDE // 512, tile)

        acts_a[1].forward()
        acts_b[1].start()
        acts_b[2].start()
        gate_up_pair(1)
        acts_a[0].finish()
        acts_a[1].finish()
        acts_b[3].start()
        gate_up(chunk(0, 1))
        cot_a[0].forward()
        got_other(C, COT)
        cot_a[1].start()
        acts_b[0].forward()
        acts_b[1].forward()
        loop(2, lambda j: gate_up(chunk(1 + 2 * j, 0)))
        cot_a[1].forward()
        acts_b[2].forward()
        acts_b[3].forward()
        cot_a[0].finish()
        cot_a[1].finish()
        cot_b[0].start()
        cot_b[1].start()
        cot_b[2].start()
        cot_b[3].start()

        def clear(i):
            gsum[span(i * 32, 32), :] = jnp.zeros((32, WIDE), F32)

        loop(2 * HID // 32, clear)

        def clear_down(i):
            dsum[span(i * 32, 32), :] = jnp.zeros((32, WIDE), F32)

        loop(HID // 32, clear_down)
        got(WD.at[:, HALF:WIDE], WTS + 2, sib)
        loop(2, lambda h: grad_hidden(chunk(0, h)))
        acts_b[0].finish()
        acts_b[1].finish()
        gate_up(chunk(2, 0))
        acts_b[2].finish()
        acts_b[3].finish()
        gate_up(chunk(2, 1))
        loop(2, lambda j: gate_up(chunk(1 + 2 * j, 1)))
        loop(2, lambda h: send_grad_hidden(chunk(0, h)))

        for part in range(2):
            sent(W2.at[part * HID:(part + 1) * HID, 0:HALF], WTS + part, sib)
        pl.semaphore_signal(credit, inc=1, device_id=sib, device_id_type=MESH)

        def share(d, h, s, i):
            send(O.at[oslot(d, h), :], RB.at[rslot(i), :], RSB + i, RSB + i, bpeer(s))

        activate(chunk(0, 0), True)
        down_step(chunk(0, 0))
        output_part(1, 0)
        output_part(3, 0)
        share(3, 0, 3, 4)
        activate(chunk(0, 1))
        down_step(chunk(0, 1))
        cot_b[0].forward()
        cot_b[1].forward()
        loop(2, lambda j: hidden_share(chunk(1 + 2 * j, 0)))
        output_part(2, 0)
        share(2, 0, 1, 0)
        loop(2, lambda j: down_step(chunk(1 + 2 * j, 0)))
        cot_b[2].forward()
        output_part(2, 1)
        share(2, 1, 3, 1)
        cot_b[3].forward()
        loop(2, lambda j: hidden_share(chunk(1 + 2 * j, 1)))
        output_part(1, 1)
        share(1, 1, 1, 3)
        down_step(chunk(1, 1))
        cot_b[0].finish()
        cot_b[1].finish()
        hidden_share(chunk(2, 0))
        down_step(chunk(2, 0))
        got(RB.at[rslot(0), :], RSB, bpeer(3))
        add_share(O, oslot(1, 0), RB, rslot(0))
        share(1, 0, 1, 2)
        output_part(3, 1)
        got(RB.at[rslot(1), :], RSB + 1, bpeer(1))
        add_share(O, oslot(3, 1), RB, rslot(1))
        share(3, 1, 3, 5)
        down_step(chunk(3, 1))
        cot_b[2].finish()
        cot_b[3].finish()
        hidden_share(chunk(2, 1))
        down_step(chunk(2, 1))

        def narrow(i):
            r = span(i * 32, 32)
            DS[r, :] = dsum[r, HALF:WIDE].astype(BF16)

        loop(HID // 32, narrow)
        send(DS, DR, GRD, GRD, sib)
        gate_step(chunk(0, 0))

        sent(O.at[oslot(2, 0), :], RSB, bpeer(1))
        sent(O.at[oslot(2, 1), :], RSB + 1, bpeer(3))

        def own_part(h):
            transpose(chunk(0, h))
            o = oslot(2, h)

            def tile(i):
                cols = span(i * 512, 512)
                O[o, cols] = nn(HT[...], WD[:, cols]).astype(BF16)

            loop(WIDE // 512, tile)

        loop(2, own_part)
        gate_step(chunk(0, 1))
        got(DR, GRD, sib)

        def down_add(i):
            r = span(i * 32, 32)
            dsum[r, 0:HALF] += DR[r, :].astype(F32)

        loop(HID // 32, down_add)
        put_down = local(dsum.at[:, 0:HALF], gd, 1)
        put_down.start()
        loop(2, lambda j: gate_step(chunk(1 + 2 * j, 0)))

        def badd(h):
            o, q, w = oslot(2, h), rslot(2 + h), rslot(4 + h)

            def tile(i):
                cols = span(i * 256, 256)
                total = O[o, cols].astype(F32) + RB[q, cols].astype(F32) + RB[w, cols].astype(F32)
                RB[q, cols] = total.astype(BF16)

            loop(WIDE // 256, tile)

        def part(d, y):
            a_ = (a + d) % 4
            return span(2 * CH + ((a_ // 2 + a // 2) % 2) * CH + (a_ % 2) * 2 * BLK + y * BLK, BLK)

        def slot(i):
            return span(i * BLK, BLK)

        got(RB.at[rslot(3), :], RSB + 3, bpeer(3))
        got(RB.at[rslot(5), :], RSB + 5, bpeer(1))
        badd(1)
        send(RB.at[part(2, 0), :], RA.at[slot(0), :], RSA, RSA, apeer(1))
        send(RB.at[part(2, 1), :], RA.at[slot(1), :], RSA + 1, RSA + 1, apeer(3))
        got(RB.at[rslot(4), :], RSB + 4, bpeer(1))
        got(RB.at[rslot(2), :], RSB + 2, bpeer(3))
        badd(0)
        send(RB.at[part(1, 1), :], RA.at[slot(3), :], RSA + 3, RSA + 3, apeer(1))
        send(RB.at[part(3, 0), :], RA.at[slot(4), :], RSA + 4, RSA + 4, apeer(3))
        gate_step(chunk(2, 0))
        got(RA.at[slot(0), :], RSA, apeer(3))
        add_share(RB, part(1, 0), RA, slot(0))
        send(RB.at[part(1, 0), :], RA.at[slot(2), :], RSA + 2, RSA + 2, apeer(1))
        got(RA.at[slot(1), :], RSA + 1, apeer(1))
        add_share(RB, part(3, 1), RA, slot(1))
        send(RB.at[part(3, 1), :], RA.at[slot(5), :], RSA + 5, RSA + 5, apeer(3))
        gate_step(chunk(1, 1))
        got(RA.at[slot(3), :], RSA + 3, apeer(3))
        got(RA.at[slot(4), :], RSA + 4, apeer(1))
        got(RA.at[slot(2), :], RSA + 2, apeer(3))
        got(RA.at[slot(5), :], RSA + 5, apeer(1))

        def aadd(y):
            def tile(i):
                cols = span(i * 512, 512)
                total = RB[part(0, y), cols].astype(F32) + RA[slot(2 + y), cols].astype(F32) + RA[slot(4 + y), cols].astype(F32)
                RB[part(0, y), cols] = total.astype(BF16)

            loop(WIDE // 512, tile)

        aadd(1 - ylo)
        send(RB.at[part(0, 1 - ylo), :], RY, RSY, RSY, lo)
        aadd(ylo)
        gate_step(chunk(3, 1))

        last = chunk(2, 1)
        slopes(last)
        pl.semaphore_wait(credit, 1)

        def piece(i):
            return span(i * 256, 256)

        def far_piece(i):
            return span(HALF + i * 256, 256)

        def give(i):
            weigh(last, far_piece(i))
            W2[:, piece(i)] = gsum[:, far_piece(i)].astype(BF16)
            send(W2.at[:, piece(i)], W2.at[:, far_piece(i)], GRU + i, GRU + i, sib)

        loop(4, give)
        loop(4, lambda i: weigh(last, piece(i)))

        got(RY, RSY, lo)
        add_share(RB, part(0, ylo), RY, pl.ds(0, BLK))
        send(RB.at[part(0, ylo), HALF:WIDE], out.at[mine, :], OUTS, OUTS, sib)
        keep = local(RB.at[part(0, ylo), 0:HALF], out.at[mine, :], 0)
        keep.start()

        def put(i):
            up = local(gsum.at[0:HID, piece(i)], gu.at[:, piece(i)], 2 + 2 * i)
            gate = local(gsum.at[HID:2 * HID, piece(i)], gg.at[:, piece(i)], 3 + 2 * i)
            return up, gate

        def take(i):
            got(W2.at[:, far_piece(i)], GRU + i, sib)
            gsum[:, piece(i)] += W2[:, far_piece(i)].astype(F32)
            for copy in put(i):
                copy.start()

        loop(4, take)

        for x_, buf, base in ((acts, A, ACTS), (cot, C, COT)):
            sent(x_.at[theirs, :], base + SIB, sib)
            sent(x_.at[mine, :], base + YLO, lo)
            sent(x_.at[theirs, :], base + YSIB, losib)
        for r in acts_a + acts_b + cot_a + cot_b:
            r.drain()
        sent(WD.at[:, 0:HALF], WTS + 2, sib)
        for k in range(8):
            sent(TO.at[k, 2 * HID:3 * HID, :], TFGH + k, hi)
        for i in range(6):
            sent(RA.at[slot(i), :], RSA + i, apeer(1))
        for i in range(2, 6):
            sent(O.at[rslot(i), :], RSB + i, bpeer(1))
        sent(RY, RSY, lo)
        sent(RB.at[part(0, ylo), HALF:WIDE], OUTS, sib)
        sent(DS, GRD, sib)
        got(out.at[theirs, :], OUTS, sib)
        keep.wait()
        put_down.wait()
        for i in range(4):
            sent(W2.at[:, i * 256:(i + 1) * 256], GRU + i, sib)
            for copy in put(i):
                copy.wait()

    pl.run_scoped(middle, pltpu.VMEM((2 * HID, WIDE), F32), pltpu.VMEM((HID, WIDE), F32))


def hand_over(*refs):
    kept, results, held, sems = refs[0:4], refs[4:8], refs[8:12], refs[12]
    pieces = [(i, j) for i in (1, 2, 3, 0) for j in range(1 if i == 0 else 2)]
    way_in, way_out = [], []
    for n, (i, j) in enumerate(pieces):
        r = pl.ds(0, 2 * BLK) if i == 0 else pl.ds(j * HID // 2, HID // 2)
        way_in.append(pltpu.make_async_copy(kept[i].at[r, :], held[i].at[r, :], sems.at[n]))
        way_out.append(pltpu.make_async_copy(held[i].at[r, :], results[i].at[r, :], sems.at[len(pieces) + n]))
    for copy in way_in:
        copy.start()
    for before, after in zip(way_in, way_out):
        before.wait()
        after.start()
    for copy in way_out:
        copy.wait()


def local_step(acts, gc, gs, uc, us, dc, ds, cot):
    anywhere = pl.BlockSpec(memory_space=pl.ANY)
    results = pl.pallas_call(
        kernel,
        out_shape=(
            jax.ShapeDtypeStruct((2 * BLK, HALF), BF16),
            jax.ShapeDtypeStruct((HID, HALF), F32),
            jax.ShapeDtypeStruct((HID, HALF), F32),
            jax.ShapeDtypeStruct((HID, HALF), F32),
        ),
        in_specs=[anywhere] * 8,
        out_specs=(anywhere,) * 4,
        scratch_shapes=[
            pltpu.VMEM((8 * CH, WIDE), BF16),
            pltpu.VMEM((8 * CH, WIDE), BF16),
            pltpu.VMEM((2 * HID, WIDE), BF16),
            pltpu.VMEM((HID, WIDE), BF16),
            pltpu.VMEM((8, 3 * HID, CH), BF16),
            pltpu.VMEM((8, 3 * HID, CH), BF16),
            pltpu.VMEM((6 * CH, WIDE), BF16),
            pltpu.VMEM((6 * CH, WIDE), BF16),
            pltpu.VMEM((6 * BLK, WIDE), BF16),
            pltpu.VMEM((BLK, WIDE), BF16),
            pltpu.VMEM((CH, HID), BF16),
            pltpu.VMEM((HID, HALF), BF16),
            pltpu.VMEM((HID, HALF), BF16),
            pltpu.SemaphoreType.DMA((NSEM,)),
            pltpu.SemaphoreType.DMA((NSEM,)),
            pltpu.SemaphoreType.DMA((10,)),
            pltpu.SemaphoreType.REGULAR,
        ],
        compiler_params=pltpu.CompilerParams(collective_id=0, has_side_effects=True, vmem_limit_bytes=63 << 20),
        name="swiglu_step",
    )(acts, gc, gs.T, uc, us.T, dc, ds.T, cot)
    return pl.pallas_call(
        hand_over,
        out_shape=tuple(jax.ShapeDtypeStruct(r.shape, r.dtype) for r in results),
        in_specs=[anywhere] * 4,
        out_specs=(anywhere,) * 4,
        scratch_shapes=[pltpu.VMEM(r.shape, r.dtype) for r in results] + [pltpu.SemaphoreType.DMA((14,))],
        compiler_params=pltpu.CompilerParams(vmem_limit_bytes=60 << 20),
        name="hand_over",
    )(*results)


def solution(mesh):
    spec = P("fsdp", "tp")
    return jax.shard_map(local_step, mesh=mesh, in_specs=(spec,) * 8, out_specs=(spec,) * 4, check_vma=False)
```

```python
import functools

import jax
import jax.numpy as jnp
from jax import lax
from jax.experimental import pallas as pl
from jax.experimental.pallas import tpu as pltpu
from jax.sharding import PartitionSpec as P

MESH = pl.DeviceIdType.MESH
F32, BF16 = jnp.float32, jnp.bfloat16
GROUP = 128
HID = 448
HALF = 1024
WIDE = 2 * HALF
BLK = 64
CH = 256

ACTS, COT, WTS, TFGU, TFGH, RSB, RSA, RSY, OUTS, GRD, GRU, PAIRS, NSEM = 0, 27, 54, 57, 65, 73, 79, 85, 86, 87, 88, 92, 94
SIB, YLO, YSIB, AOWN, ALO, BPAIR = 0, 1, 2, 3, 7, 11


def nt(left, right):
    return lax.dot_general(left, right, (((1,), (1,)), ((), ())), preferred_element_type=F32)


def nn(left, right):
    return lax.dot_general(left, right, (((1,), (0,)), ((), ())), preferred_element_type=F32)


def kernel(acts, gc, gs, uc, us, dc, ds, cot, out, gg, gu, gd,
           A, C, W2, WD, TO, TR, O, RB, RA, RY, HT, DS, DR, ssem, rsem, lsem, credit):
    f, t = lax.axis_index("fsdp"), lax.axis_index("tp")
    x, ylo, z = f % 4, (f // 4) % 2, f // 8
    yhi, c = t // 2, t % 2
    a = x * (1 - c) + z * c
    b = z * (1 - c) + x * c

    def dev(x_, ylo_, z_, yhi_, c_):
        return (z_ * 8 + ylo_ * 4 + x_, yhi_ * 2 + c_)

    def apeer(d):
        return dev((x + d * (1 - c)) % 4, ylo, (z + d * c) % 4, yhi, c)

    def bpeer(d):
        return dev((x + d * c) % 4, ylo, (z + d * (1 - c)) % 4, yhi, c)

    sib = dev(x, ylo, z, yhi, 1 - c)
    lo = dev(x, 1 - ylo, z, yhi, c)
    losib = dev(x, 1 - ylo, z, yhi, 1 - c)
    hi = dev(x, ylo, z, 1 - yhi, c)

    def rc(src, dst, s, r, to):
        return pltpu.make_async_remote_copy(src_ref=src, dst_ref=dst, send_sem=ssem.at[s], recv_sem=rsem.at[r],
                                            device_id=to, device_id_type=MESH)

    def send(src, dst, s, r, to):
        rc(src, dst, s, r, to).start()

    def got(dst, r, to):
        rc(dst, dst, 0, r, to).wait_recv()

    def sent(src, s, to):
        rc(src, src, s, 0, to).wait_send()

    def span(row, n):
        return pl.ds(pl.multiple_of(row, n), n)

    def blk(a_, ylo_):
        return span(((b * 4 + a_) * 2 + ylo_) * BLK, BLK)

    def chunk(d, h):
        return ((b + d) % 4) * 2 + (a // 2 + h) % 2

    def rows(k):
        return pl.ds(pl.multiple_of(k * CH, CH), CH)

    mine = pl.ds(pl.multiple_of(c * BLK, BLK), BLK)
    theirs = pl.ds(pl.multiple_of((1 - c) * BLK, BLK), BLK)
    own = blk(a, ylo)
    other = blk(a, 1 - ylo)
    sibs = pl.ds(pl.multiple_of(((a * 4 + b) * 2 + ylo) * BLK, BLK), BLK)

    def local(src, dst, i):
        return pltpu.make_async_copy(src, dst, lsem.at[i])

    class Round:
        def __init__(self, buf, row, n, base, peer):
            self.buf, self.row, self.n, self.base, self.peer = buf, row, n, base, peer

        def view(self, d, half=None):
            if half is None:
                return self.buf.at[span(self.row(d), self.n), :]
            return self.buf.at[span(self.row(d) + half * (self.n // 2), self.n // 2), :]

        def start(self):
            send(self.view(0), self.view(0), self.base, self.base + 1, self.peer(1))
            send(self.view(0), self.view(0), self.base + 1, self.base, self.peer(3))

        def forward(self):
            got(self.view(1), self.base, self.peer(1))
            send(self.view(1, 0), self.view(1, 0), self.base + 2, self.base + 2, self.peer(3))
            got(self.view(3), self.base + 1, self.peer(3))
            send(self.view(3, 1), self.view(3, 1), self.base + 3, self.base + 3, self.peer(1))

        def finish(self):
            got(self.view(2, 0), self.base + 2, self.peer(1))
            got(self.view(2, 1), self.base + 3, self.peer(3))

        def drain(self):
            sent(self.view(0), self.base, self.peer(1))
            sent(self.view(0), self.base + 1, self.peer(3))
            sent(self.view(1, 0), self.base + 2, self.peer(3))
            sent(self.view(3, 1), self.base + 3, self.peer(1))

    opposite = (a + 2) % 4
    order = (a, a + 1 - 2 * (a % 2), opposite + 1 - 2 * (opposite % 2), opposite)

    def rounds(buf, base):
        def around_a(ylo_, sem):
            return Round(buf, lambda d: ((b * 4 + (a + d) % 4) * 2 + ylo_) * BLK, BLK, base + sem, apeer)

        def around_b(i):
            return Round(buf, lambda d: (((b + d) % 4) * 4 + order[i]) * 2 * BLK, 2 * BLK, base + BPAIR + 4 * i, bpeer)

        return [around_a(ylo, AOWN), around_a(1 - ylo, ALO)], [around_b(i) for i in range(4)]

    acts_a, acts_b = rounds(A, ACTS)
    cot_a, cot_b = rounds(C, COT)

    def got_other(buf, base):
        got(buf.at[other, 0:HALF], base + YLO, lo)
        got(buf.at[other, HALF:WIDE], base + YSIB, losib)

    def opening(codes, scales, turned):
        loads = [local(gc, codes.at[0], 0), local(gs, turned.at[0], 1), local(uc, codes.at[1], 2), local(us, turned.at[1], 3),
                 local(ds, turned.at[2], 4)]
        own_acts = local(acts.at[mine, :], A.at[own, 0:HALF], 5)
        own_cot = local(cot.at[mine, :], C.at[own, 0:HALF], 6)
        for load in (own_acts, loads[0], loads[1], own_cot, loads[2], loads[3], loads[4]):
            load.start()

        barrier = pltpu.get_barrier_semaphore()
        peers = [sib, lo, losib, hi, apeer(1), apeer(3), bpeer(1), bpeer(3)]
        for peer in peers:
            pl.semaphore_signal(barrier, inc=1, device_id=peer, device_id_type=MESH)
        pl.semaphore_wait(barrier, len(peers))

        for x_, buf, base in ((acts, A, ACTS), (cot, C, COT)):
            send(x_.at[theirs, :], buf.at[sibs, HALF:WIDE], base + SIB, base + SIB, sib)
            send(x_.at[mine, :], buf.at[own, 0:HALF], base + YLO, base + YLO, lo)
            send(x_.at[theirs, :], buf.at[sibs, HALF:WIDE], base + YSIB, base + YSIB, losib)
        own_acts.wait()
        got(A.at[own, HALF:WIDE], ACTS + SIB, sib)
        acts_a[0].start()
        own_cot.wait()
        got(C.at[own, HALF:WIDE], COT + SIB, sib)
        cot_a[0].start()

        def dequantize(slot, which, w, first):
            scales[which] = jnp.transpose(turned[which])

            def tile(i, _):
                r = span(i * 32, 32)
                rw = span(first + i * 32, 32)
                for g in range(HALF // GROUP):
                    cols = slice(g * GROUP, (g + 1) * GROUP)
                    w[rw, cols] = (codes[slot, r, cols].astype(F32) * scales[which, r, g:g + 1]).astype(BF16)
                return 0

            lax.fori_loop(0, HID // 32, tile, 0)

        down = local(dc, codes.at[0], 7)
        loads[0].wait()
        loads[1].wait()
        dequantize(0, 0, W2, 0)
        send(W2.at[0:HID, 0:HALF], W2.at[0:HID, HALF:WIDE], WTS, WTS, sib)
        down.start()
        acts_a[0].forward()
        loads[2].wait()
        loads[3].wait()
        dequantize(1, 1, W2, HID)
        send(W2.at[HID:2 * HID, 0:HALF], W2.at[HID:2 * HID, HALF:WIDE], WTS + 1, WTS + 1, sib)
        got_other(A, ACTS)
        acts_a[1].start()
        acts_b[0].start()
        for part in range(2):
            got(W2.at[part * HID:(part + 1) * HID, HALF:WIDE], WTS + part, sib)
        gate_up_pair(0)
        loads[4].wait()
        down.wait()
        dequantize(0, 2, WD, 0)
        send(WD.at[:, 0:HALF], WD.at[:, HALF:WIDE], WTS + 2, WTS + 2, sib)

    def gate_up(k):
        block = A[rows(k), :]
        for part in range(2):
            r = slice(part * HID, (part + 1) * HID)
            TO[k, r, :] = nt(W2[r, :], block).astype(BF16)
        send(TO.at[k, 0:2 * HID, :], TR.at[k, 0:2 * HID, :], TFGU + k, TFGU + k, hi)

    def pair_cols(i):
        return span(((order[i] % 2) * 2 * BLK), 2 * BLK)

    def gate_up_pair(i):
        k, cols = chunk(0, 0), pair_cols(i)
        block = A[span((b * 4 + order[i]) * 2 * BLK, 2 * BLK), :]
        for part in range(2):
            r = slice(part * HID, (part + 1) * HID)
            TO[k, r, cols] = nt(W2[r, :], block).astype(BF16)
        send(TO.at[k, 0:2 * HID, cols], TR.at[k, 0:2 * HID, cols], PAIRS + i, PAIRS + i, hi)

    pl.run_scoped(opening, pltpu.VMEM((2, HID, HALF), jnp.int32), pltpu.VMEM((3, HID, HALF // GROUP), F32),
                  pltpu.VMEM((3, HALF // GROUP, HID), F32))

    def grad_hidden(k):
        TO[k, 2 * HID:3 * HID, :] = nt(WD[...], C[rows(k), :]).astype(BF16)

    def send_grad_hidden(k):
        send(TO.at[k, 2 * HID:3 * HID, :], TR.at[k, 2 * HID:3 * HID, :], TFGH + k, TFGH + k, hi)

    def hidden_share(k):
        grad_hidden(k)
        send_grad_hidden(k)

    def activate(k, pairs=False):
        if pairs:
            for i in range(2):
                got(TR.at[k, 0:2 * HID, pair_cols(i)], PAIRS + i, hi)
                sent(TO.at[k, 0:2 * HID, pair_cols(i)], PAIRS + i, hi)
        else:
            got(TR.at[k, 0:2 * HID, :], TFGU + k, hi)
            sent(TO.at[k, 0:2 * HID, :], TFGU + k, hi)

        def tile(i, _):
            r, q = span(i * 32, 32), span(HID + i * 32, 32)
            gate = TO[k, r, :].astype(F32) + TR[k, r, :].astype(F32)
            up = TO[k, q, :].astype(F32) + TR[k, q, :].astype(F32)
            s = 1.0 / (1.0 + jnp.exp(-gate))
            silu = gate * s
            TO[k, r, :] = (silu * up).astype(BF16)
            TR[k, r, :] = silu.astype(BF16)
            TR[k, q, :] = (up * (s * (1.0 + gate * (1.0 - s)))).astype(BF16)
            return 0

        lax.fori_loop(0, HID // 32, tile, 0)

    def transpose(k):
        HT[...] = jnp.transpose(TO[k, 0:HID, :].astype(F32)).astype(BF16)

    def oslot(d, h):
        return span(((d - 1) * 2 + h) * CH, CH)

    def rslot(i):
        return span(i * CH, CH)

    def output_part(d, h):
        k = chunk(d, h)
        activate(k)
        transpose(k)
        o = oslot(d, h)

        def tile(i, _):
            cols = span(i * 512, 512)
            O[o, cols] = nn(HT[...], WD[:, cols]).astype(BF16)
            return 0

        lax.fori_loop(0, WIDE // 512, tile, 0)

    def loop(n, body):
        lax.fori_loop(0, n, lambda i, _: (body(i), 0)[1], 0)

    def middle(gsum, dsum):
        def down_step(k):
            def tile(i):
                cols = span(i * 512, 512)
                dsum[:, cols] += nn(TO[k, 0:HID, :], C[rows(k), cols])

            loop(WIDE // 512, tile)

        def slopes(k):
            got(TR.at[k, 2 * HID:3 * HID, :], TFGH + k, hi)

            def tile(i):
                r, q, w = span(i * 32, 32), span(HID + i * 32, 32), span(2 * HID + i * 32, 32)
                grad = TO[k, w, :].astype(F32) + TR[k, w, :].astype(F32)
                TR[k, r, :] = (grad * TR[k, r, :].astype(F32)).astype(BF16)
                TR[k, q, :] = (grad * TR[k, q, :].astype(F32)).astype(BF16)

            loop(HID // 32, tile)

        def weigh(k, cols):
            gsum[:, cols] += nn(TR[k, 0:2 * HID, :], A[rows(k), cols])

        def gate_step(k):
            slopes(k)
            loop(WIDE // 256, lambda i: weigh(k, span(i * 256, 256)))

        def add_share(buf, r, other_buf, q):
            def tile(i):
                cols = span(i * 512, 512)
                buf[r, cols] = (buf[r, cols].astype(F32) + other_buf[q, cols].astype(F32)).astype(BF16)

            loop(WIDE // 512, tile)

        acts_a[1].forward()
        acts_b[1].start()
        acts_b[2].start()
        gate_up_pair(1)
        acts_a[0].finish()
        acts_a[1].finish()
        acts_b[3].start()
        gate_up(chunk(0, 1))
        cot_a[0].forward()
        got_other(C, COT)
        cot_a[1].start()
        acts_b[0].forward()
        acts_b[1].forward()
        loop(2, lambda j: gate_up(chunk(1 + 2 * j, 0)))
        cot_a[1].forward()
        acts_b[2].forward()
        acts_b[3].forward()
        cot_a[0].finish()
        cot_a[1].finish()
        cot_b[0].start()
        cot_b[1].start()
        cot_b[2].start()
        cot_b[3].start()

        def clear(i):
            gsum[span(i * 32, 32), :] = jnp.zeros((32, WIDE), F32)

        loop(2 * HID // 32, clear)

        def clear_down(i):
            dsum[span(i * 32, 32), :] = jnp.zeros((32, WIDE), F32)

        loop(HID // 32, clear_down)
        got(WD.at[:, HALF:WIDE], WTS + 2, sib)
        loop(2, lambda h: grad_hidden(chunk(0, h)))
        acts_b[0].finish()
        acts_b[1].finish()
        gate_up(chunk(2, 0))
        acts_b[2].finish()
        acts_b[3].finish()
        gate_up(chunk(2, 1))
        loop(2, lambda j: gate_up(chunk(1 + 2 * j, 1)))
        loop(2, lambda h: send_grad_hidden(chunk(0, h)))

        for part in range(2):
            sent(W2.at[part * HID:(part + 1) * HID, 0:HALF], WTS + part, sib)
        pl.semaphore_signal(credit, inc=1, device_id=sib, device_id_type=MESH)

        def share(d, h, s, i):
            send(O.at[oslot(d, h), :], RB.at[rslot(i), :], RSB + i, RSB + i, bpeer(s))

        activate(chunk(0, 0), True)
        down_step(chunk(0, 0))
        output_part(1, 0)
        output_part(3, 0)
        share(3, 0, 3, 4)
        activate(chunk(0, 1))
        down_step(chunk(0, 1))
        cot_b[0].forward()
        cot_b[1].forward()
        loop(2, lambda j: hidden_share(chunk(1 + 2 * j, 0)))
        output_part(2, 0)
        share(2, 0, 1, 0)
        loop(2, lambda j: down_step(chunk(1 + 2 * j, 0)))
        cot_b[2].forward()
        output_part(2, 1)
        share(2, 1, 3, 1)
        cot_b[3].forward()
        loop(2, lambda j: hidden_share(chunk(1 + 2 * j, 1)))
        output_part(1, 1)
        share(1, 1, 1, 3)
        down_step(chunk(1, 1))
        cot_b[0].finish()
        cot_b[1].finish()
        hidden_share(chunk(2, 0))
        down_step(chunk(2, 0))
        got(RB.at[rslot(0), :], RSB, bpeer(3))
        add_share(O, oslot(1, 0), RB, rslot(0))
        share(1, 0, 1, 2)
        output_part(3, 1)
        got(RB.at[rslot(1), :], RSB + 1, bpeer(1))
        add_share(O, oslot(3, 1), RB, rslot(1))
        share(3, 1, 3, 5)
        down_step(chunk(3, 1))
        cot_b[2].finish()
        cot_b[3].finish()
        hidden_share(chunk(2, 1))
        down_step(chunk(2, 1))

        def narrow(i):
            r = span(i * 32, 32)
            DS[r, :] = dsum[r, HALF:WIDE].astype(BF16)

        loop(HID // 32, narrow)
        send(DS, DR, GRD, GRD, sib)
        gate_step(chunk(0, 0))

        sent(O.at[oslot(2, 0), :], RSB, bpeer(1))
        sent(O.at[oslot(2, 1), :], RSB + 1, bpeer(3))

        def own_part(h):
            transpose(chunk(0, h))
            o = oslot(2, h)

            def tile(i):
                cols = span(i * 512, 512)
                O[o, cols] = nn(HT[...], WD[:, cols]).astype(BF16)

            loop(WIDE // 512, tile)

        loop(2, own_part)
        gate_step(chunk(0, 1))
        got(DR, GRD, sib)

        def down_add(i):
            r = span(i * 32, 32)
            dsum[r, 0:HALF] += DR[r, :].astype(F32)

        loop(HID // 32, down_add)
        put_down = local(dsum.at[:, 0:HALF], gd, 1)
        put_down.start()
        loop(2, lambda j: gate_step(chunk(1 + 2 * j, 0)))

        def badd(h):
            o, q, w = oslot(2, h), rslot(2 + h), rslot(4 + h)

            def tile(i):
                cols = span(i * 256, 256)
                total = O[o, cols].astype(F32) + RB[q, cols].astype(F32) + RB[w, cols].astype(F32)
                RB[q, cols] = total.astype(BF16)

            loop(WIDE // 256, tile)

        def part(d, y):
            a_ = (a + d) % 4
            return span(2 * CH + ((a_ // 2 + a // 2) % 2) * CH + (a_ % 2) * 2 * BLK + y * BLK, BLK)

        def slot(i):
            return span(i * BLK, BLK)

        got(RB.at[rslot(3), :], RSB + 3, bpeer(3))
        got(RB.at[rslot(5), :], RSB + 5, bpeer(1))
        badd(1)
        send(RB.at[part(2, 0), :], RA.at[slot(0), :], RSA, RSA, apeer(1))
        send(RB.at[part(2, 1), :], RA.at[slot(1), :], RSA + 1, RSA + 1, apeer(3))
        got(RB.at[rslot(4), :], RSB + 4, bpeer(1))
        got(RB.at[rslot(2), :], RSB + 2, bpeer(3))
        badd(0)
        send(RB.at[part(1, 1), :], RA.at[slot(3), :], RSA + 3, RSA + 3, apeer(1))
        send(RB.at[part(3, 0), :], RA.at[slot(4), :], RSA + 4, RSA + 4, apeer(3))
        gate_step(chunk(1, 1))
        got(RA.at[slot(0), :], RSA, apeer(3))
        add_share(RB, part(1, 0), RA, slot(0))
        send(RB.at[part(1, 0), :], RA.at[slot(2), :], RSA + 2, RSA + 2, apeer(1))
        got(RA.at[slot(1), :], RSA + 1, apeer(1))
        add_share(RB, part(3, 1), RA, slot(1))
        send(RB.at[part(3, 1), :], RA.at[slot(5), :], RSA + 5, RSA + 5, apeer(3))
        gate_step(chunk(3, 1))
        got(RA.at[slot(3), :], RSA + 3, apeer(3))
        got(RA.at[slot(4), :], RSA + 4, apeer(1))
        got(RA.at[slot(2), :], RSA + 2, apeer(3))
        got(RA.at[slot(5), :], RSA + 5, apeer(1))

        def aadd(y):
            def tile(i):
                cols = span(i * 512, 512)
                total = RB[part(0, y), cols].astype(F32) + RA[slot(2 + y), cols].astype(F32) + RA[slot(4 + y), cols].astype(F32)
                RB[part(0, y), cols] = total.astype(BF16)

            loop(WIDE // 512, tile)

        aadd(1 - ylo)
        send(RB.at[part(0, 1 - ylo), :], RY, RSY, RSY, lo)
        aadd(ylo)
        gate_step(chunk(2, 0))

        last = chunk(2, 1)
        slopes(last)
        pl.semaphore_wait(credit, 1)

        def piece(i):
            return span(i * 256, 256)

        def far_piece(i):
            return span(HALF + i * 256, 256)

        def give(i):
            weigh(last, far_piece(i))
            W2[:, piece(i)] = gsum[:, far_piece(i)].astype(BF16)
            send(W2.at[:, piece(i)], W2.at[:, far_piece(i)], GRU + i, GRU + i, sib)

        loop(4, give)
        loop(4, lambda i: weigh(last, piece(i)))

        def put(i):
            up = local(gsum.at[0:HID, piece(i)], gu.at[:, piece(i)], 2 + 2 * i)
            gate = local(gsum.at[HID:2 * HID, piece(i)], gg.at[:, piece(i)], 3 + 2 * i)
            return up, gate

        def take(i):
            got(W2.at[:, far_piece(i)], GRU + i, sib)
            gsum[:, piece(i)] += W2[:, far_piece(i)].astype(F32)
            for copy in put(i):
                copy.start()

        loop(4, take)

        got(RY, RSY, lo)
        add_share(RB, part(0, ylo), RY, pl.ds(0, BLK))
        send(RB.at[part(0, ylo), HALF:WIDE], out.at[mine, :], OUTS, OUTS, sib)
        keep = local(RB.at[part(0, ylo), 0:HALF], out.at[mine, :], 0)
        keep.start()

        for x_, buf, base in ((acts, A, ACTS), (cot, C, COT)):
            sent(x_.at[theirs, :], base + SIB, sib)
            sent(x_.at[mine, :], base + YLO, lo)
            sent(x_.at[theirs, :], base + YSIB, losib)
        for r in acts_a + acts_b + cot_a + cot_b:
            r.drain()
        sent(WD.at[:, 0:HALF], WTS + 2, sib)
        for k in range(8):
            sent(TO.at[k, 2 * HID:3 * HID, :], TFGH + k, hi)
        for i in range(6):
            sent(RA.at[slot(i), :], RSA + i, apeer(1))
        for i in range(2, 6):
            sent(O.at[rslot(i), :], RSB + i, bpeer(1))
        sent(RY, RSY, lo)
        sent(RB.at[part(0, ylo), HALF:WIDE], OUTS, sib)
        sent(DS, GRD, sib)
        got(out.at[theirs, :], OUTS, sib)
        keep.wait()
        put_down.wait()
        for i in range(4):
            sent(W2.at[:, i * 256:(i + 1) * 256], GRU + i, sib)
            for copy in put(i):
                copy.wait()

    pl.run_scoped(middle, pltpu.VMEM((2 * HID, WIDE), F32), pltpu.VMEM((HID, WIDE), F32))


def hand_over(*refs):
    kept, results, held, sems = refs[0:4], refs[4:8], refs[8:12], refs[12]
    pieces = [(i, j) for i in (1, 2, 3, 0) for j in range(1 if i == 0 else 2)]
    way_in, way_out = [], []
    for n, (i, j) in enumerate(pieces):
        r = pl.ds(0, 2 * BLK) if i == 0 else pl.ds(j * HID // 2, HID // 2)
        way_in.append(pltpu.make_async_copy(kept[i].at[r, :], held[i].at[r, :], sems.at[n]))
        way_out.append(pltpu.make_async_copy(held[i].at[r, :], results[i].at[r, :], sems.at[len(pieces) + n]))
    for copy in way_in:
        copy.start()
    for before, after in zip(way_in, way_out):
        before.wait()
        after.start()
    for copy in way_out:
        copy.wait()


def local_step(acts, gc, gs, uc, us, dc, ds, cot):
    anywhere = pl.BlockSpec(memory_space=pl.ANY)
    results = pl.pallas_call(
        kernel,
        out_shape=(
            jax.ShapeDtypeStruct((2 * BLK, HALF), BF16),
            jax.ShapeDtypeStruct((HID, HALF), F32),
            jax.ShapeDtypeStruct((HID, HALF), F32),
            jax.ShapeDtypeStruct((HID, HALF), F32),
        ),
        in_specs=[anywhere] * 8,
        out_specs=(anywhere,) * 4,
        scratch_shapes=[
            pltpu.VMEM((8 * CH, WIDE), BF16),
            pltpu.VMEM((8 * CH, WIDE), BF16),
            pltpu.VMEM((2 * HID, WIDE), BF16),
            pltpu.VMEM((HID, WIDE), BF16),
            pltpu.VMEM((8, 3 * HID, CH), BF16),
            pltpu.VMEM((8, 3 * HID, CH), BF16),
            pltpu.VMEM((6 * CH, WIDE), BF16),
            pltpu.VMEM((6 * CH, WIDE), BF16),
            pltpu.VMEM((6 * BLK, WIDE), BF16),
            pltpu.VMEM((BLK, WIDE), BF16),
            pltpu.VMEM((CH, HID), BF16),
            pltpu.VMEM((HID, HALF), BF16),
            pltpu.VMEM((HID, HALF), BF16),
            pltpu.SemaphoreType.DMA((NSEM,)),
            pltpu.SemaphoreType.DMA((NSEM,)),
            pltpu.SemaphoreType.DMA((10,)),
            pltpu.SemaphoreType.REGULAR,
        ],
        compiler_params=pltpu.CompilerParams(collective_id=0, has_side_effects=True, vmem_limit_bytes=63 << 20),
        name="swiglu_step",
    )(acts, gc, gs.T, uc, us.T, dc, ds.T, cot)
    return pl.pallas_call(
        hand_over,
        out_shape=tuple(jax.ShapeDtypeStruct(r.shape, r.dtype) for r in results),
        in_specs=[anywhere] * 4,
        out_specs=(anywhere,) * 4,
        scratch_shapes=[pltpu.VMEM(r.shape, r.dtype) for r in results] + [pltpu.SemaphoreType.DMA((14,))],
        compiler_params=pltpu.CompilerParams(vmem_limit_bytes=60 << 20),
        name="hand_over",
    )(*results)


def solution(mesh):
    spec = P("fsdp", "tp")
    return jax.shard_map(local_step, mesh=mesh, in_specs=(spec,) * 8, out_specs=(spec,) * 4, check_vma=False)
```
